128 devices in a mesh: band: 32 (over z_hi, x, y), bus: 4 (over z_lo, core).
Axes of the slice: x: 4, y: 4, z: 4 (z_hi: 2, z_lo: 2; z = z_hi * 2 + z_lo), core: 2. Of those that a mesh axis runs over, the one named last changes fastest.
Arguments:
- dispatch0: float32 [64, 20480], P(None, ('band', 'bus')), may hold values from 0 to 1
- cost_lin: float32 [20480], P(('band', 'bus')), may hold values from -1 to 1
- cost_quad: float32 [20480], P(('band', 'bus')), may hold values from 0.5 to 4
- gen_max: float32 [20480], P(('band', 'bus')), may hold values from 0.5 to 2
- bus_map: int32 [20480], P(('band', 'bus')), may hold values from 0 to 98303, as said below
- demand: float32 [64, 4, 24576], P(None, 'bus', 'band'), may hold values from -6 to 6
- ptdf: float32 [8192, 98304], P('band', 'bus'), may hold values from -0.01953125 to 0.01953125
- line_price0: float32 [64, 8192], P(None, 'band'), may hold values from -3 to 3
- flow_max: float32 [8192], P('band'), may hold values from 0.3 to 3
Outputs:
- dispatch: float32 [64, 20480], P(None, ('band', 'bus'))
- line_price: float32 [64, 8192], P(None, 'band')
The draws below stay inside these ranges and needn't reach their ends.
Inputs may be any that keep to these rules, and one draw needn't show every extreme that they name: `bus_map`: call bus 24576 * j + 768 * i + k with 0 <= k < 768 a bus of sub-block (i, j). Among the 160 generators of one aligned block (generators 160 * d to 160 * d + 159), at most 3 are sited in one sub-block, and one sub-block holds exactly 3 generators of every block.
All inputs are finite; a program needn't handle non-finite values.
Results may differ from the reference program's by a relative error of at most 0.0003.
Values sent between devices are 32-bit elements; how exact they have to be, the bound alone decides.
No kernel may reach another device: no remote copies, remote signals or barrier semaphores. Data moves between devices by JAX's collectives and lax.ppermute only.
A program may use at most 128 MiB of HBM per device.

```python
import math
import jax
import jax.numpy as jnp
from jax import lax

BUS_DEV = 24576
GEN_DEV = 160
S = 64
ITERS = 2
SUB = 768
BUSES = 98304
LINES = 8192
GENS = 20480
CAP = 3
N_BUS = 4
DEVICES = 128


def draw_bus_map(key, part):
    hot_key, rest_key = jax.random.split(jax.random.fold_in(key, 7))
    hot = jax.random.randint(hot_key, (), 0, DEVICES).astype(jnp.int32)

    def one_block(block_key):
        first_key, second_key, third_key = jax.random.split(block_key, 3)
        slots = jax.random.permutation(first_key, (DEVICES - 1) * CAP)[:GEN_DEV - CAP].astype(jnp.int32)
        other = slots // CAP
        other = other + (other >= hot).astype(jnp.int32)
        owner = jnp.concatenate([jnp.full((CAP,), hot, jnp.int32), other])
        owner = jax.random.permutation(second_key, owner).astype(jnp.int32)
        within = jax.random.randint(third_key, (GEN_DEV,), 0, SUB).astype(jnp.int32)
        return owner % N_BUS * BUS_DEV + owner // N_BUS * SUB + within
    block_keys = jax.random.split(rest_key, DEVICES)
    return jax.vmap(one_block)(block_keys).reshape(-1).astype(jnp.int32)


def levels(stream_key, dims, pieces, smallest, top_value):
    gain = 1.0
    for axis_at, shards_of in pieces:
        heights = jax.random.uniform(jax.random.fold_in(jax.random.fold_in(stream_key, 6), axis_at), (shards_of,), jnp.float32, smallest / len(pieces), top_value / len(pieces))
        gain = gain * jnp.repeat(jnp.exp(heights), dims[axis_at] // shards_of).reshape((-1,) + (1,) * (len(dims) - 1 - axis_at))
    return gain


def noise(own_key, extent, width, reach, cuts=(), dtype=jnp.bfloat16):
    array = jax.random.normal(own_key, extent, jnp.float32) * width
    if len(cuts) > 0:
        array = levels(own_key, extent, cuts, -0.22, 0.18) * array
    return jnp.clip(array, min=-reach, max=reach).astype(dtype)


def setup_inputs(seed: int = 0) -> dict:
    splits = jax.random.split(jax.random.key(seed), 10)
    dispatch0 = jnp.clip(1.0 * jax.random.uniform(splits[0], (S, GENS), jnp.float32) ** levels(splits[0], (S, GENS), ((1, 128),), -0.2, 0.2), 0.0, 1.0)
    cost_lin = jnp.clip(jax.random.uniform(splits[1], (GENS,), jnp.float32, -1.0, 1.0) * levels(splits[1], (GENS,), ((0, 128),), -0.4, 0.0), -1.0, 1.0)
    cost_quad = jnp.clip(jnp.exp(math.log(4.0) - 2.0794415 * jax.random.uniform(splits[2], (GENS,), jnp.float32) ** levels(splits[2], (GENS,), ((0, 128),), -0.2, 0.2)), 0.5, 4.0)
    gen_max = jnp.clip(0.5 + 1.5 * jax.random.uniform(splits[3], (GENS,), jnp.float32) ** levels(splits[3], (GENS,), ((0, 128),), -0.2, 0.2), 0.5, 2.0)
    bus_map = draw_bus_map(jax.random.fold_in(splits[9], 71), 0)
    demand = noise(splits[5], (S, N_BUS, BUS_DEV), 1.0, 6.0, ((1, 4), (2, 32)), jnp.float32)
    ptdf = noise(splits[6], (LINES, BUSES), BUSES ** -0.5, 0.01953125, ((0, 32), (1, 4)), jnp.float32)
    line_price0 = noise(splits[7], (S, LINES), 0.5, 3.0, ((1, 32),), jnp.float32)
    flow_max = jnp.clip(jnp.exp(math.log(3.0) - 2.3025851 * jax.random.uniform(splits[8], (LINES,), jnp.float32) ** levels(splits[8], (LINES,), ((0, 32),), -0.2, 0.2)), 0.3, 3.0)
    return dict(dispatch0=dispatch0, cost_lin=cost_lin, cost_quad=cost_quad, gen_max=gen_max, bus_map=bus_map, demand=demand, ptdf=ptdf, line_price0=line_price0, flow_max=flow_max)


primal_step = 0.5
dual_step = 1.0


def reference(dispatch0, cost_lin, cost_quad, gen_max, bus_map, demand, ptdf, line_price0, flow_max):
    dispatch = dispatch0
    line_price = line_price0
    load = demand.reshape(S, BUSES)
    bound = dual_step * flow_max
    for iteration in range(ITERS):
        injection = jnp.zeros((S, BUSES), jnp.float32).at[:, bus_map].add(dispatch) - load
        flow = jnp.dot(injection, ptdf.T, precision=lax.Precision.HIGHEST, preferred_element_type=jnp.float32)
        trial = line_price + dual_step * flow
        price_next = trial - jnp.clip(trial, -bound, bound)
        reflected = 2.0 * price_next - line_price
        bus_price = jnp.dot(reflected, ptdf, precision=lax.Precision.HIGHEST, preferred_element_type=jnp.float32)
        unit_price = bus_price[:, bus_map]
        dispatch = jnp.clip((dispatch - primal_step * (cost_lin[None, :] + unit_price)) / (1.0 + primal_step * cost_quad[None, :]), 0.0, gen_max[None, :])
        line_price = price_next
    return dispatch, line_price
```

```python
import jax
import jax.numpy as jnp
from jax import lax
from jax.experimental import pallas as pl
from jax.experimental.pallas import tpu as pltpu
from jax.sharding import PartitionSpec as P

ITERS = 2
S = 64
HALF = 32
SUB = 768
BUS_DEV = 24576
CAP = 3
DEVICES = 128
N_BUS = 4
N_BAND = 32
SLOTS = CAP * DEVICES
GEN_DEV = 160
LINES_DEV = 256
LOAD_ROWS = SUB // 128 * HALF
SLOT_ROWS = CAP * HALF

primal_step = 0.5
dual_step = 1.0

NZ, NX, NY = 2, 4, 4


def band_index(z, x, y):
    return (z * NX + x) * NY + y


def shift(dz, dx, dy):
    return [
        (band_index(z, x, y), band_index((z + dz) % NZ, (x + dx) % NX, (y + dy) % NY))
        for z in range(NZ)
        for x in range(NX)
        for y in range(NY)
    ]


def moved(a, dz, dx, dy):
    return lax.ppermute(a, "band", shift(dz, dx, dy))


def ring_x(r):
    return (0, r, 0)


def ring_y(r):
    return (0, 0, r)


def gather_band(a, b):
    both = jnp.stack([a, b])
    other = moved(both, 1, 0, 0)
    out = []
    for k, (first, second) in enumerate(((ring_x, ring_y), (ring_y, ring_x))):
        pair = jnp.concatenate([both[k], other[k]], axis=0)
        eight = jnp.concatenate(
            [pair] + [moved(pair, *first(-r)) for r in (1, 2, 3)], axis=0
        )
        out.append([eight] + [moved(eight, *second(-r)) for r in (1, 2, 3)])
    return out


def sum_band(chunks_a, chunks_b):
    pairs = []
    for chunks, first, second in (
        (chunks_a, ring_x, ring_y),
        (chunks_b, ring_y, ring_x),
    ):
        got = [moved(chunks[r], *second(r)) for r in (2, 1, 3)]
        eight = chunks[0] + got[0] + got[1] + got[2]
        n = eight.shape[0] // 4
        parts = [eight[r * n : (r + 1) * n] for r in range(4)]
        got = [moved(parts[r], *first(r)) for r in (2, 1, 3)]
        pairs.append(parts[0] + got[0] + got[1] + got[2])
    n = pairs[0].shape[0] // 2
    got = moved(jnp.stack([p[n:] for p in pairs]), 1, 0, 0)
    return pairs[0][:n] + got[0], pairs[1][:n] + got[1]


def split(v):
    hi = v.astype(jnp.bfloat16)
    lo = (v - hi.astype(jnp.float32)).astype(jnp.bfloat16)
    return hi, lo


NT = (((1,), (1,)), ((), ()))
NN = (((1,), (0,)), ((), ()))


def three_pass(x, w_hi, w_lo, dims):
    x_hi, x_lo = split(x)
    n = x.shape[0]
    y = lax.dot_general(
        jnp.concatenate([x_hi, x_lo], axis=0), w_hi, dims, preferred_element_type=jnp.float32
    )
    return y[:n] + (
        y[n:] + lax.dot_general(x_hi, w_lo, dims, preferred_element_type=jnp.float32)
    )


def lanes(ref, count):
    return jnp.concatenate(
        [ref[k * HALF : (k + 1) * HALF, :] for k in range(count)], axis=1
    )


def load_flow_kernel(idx_ref, x_ref, w_ref, o_ref):
    @pl.when(pl.program_id(0) == 0)
    def _():
        o_ref[...] = jnp.zeros_like(o_ref)

    w_hi, w_lo = split(w_ref[...])
    o_ref[...] += three_pass(lanes(x_ref, SUB // 128), w_hi, w_lo, NT)


def load_flow(x, ptdf, idx):
    steps = idx.shape[0]
    return pl.pallas_call(
        load_flow_kernel,
        grid_spec=pltpu.PrefetchScalarGridSpec(
            num_scalar_prefetch=1,
            grid=(steps,),
            in_specs=[
                pl.BlockSpec((LOAD_ROWS, 128), lambda i, idx: (i, 0)),
                pl.BlockSpec((LINES_DEV, SUB), lambda i, idx: (0, idx[i])),
            ],
            out_specs=pl.BlockSpec((HALF, LINES_DEV), lambda i, idx: (0, 0)),
        ),
        out_shape=jax.ShapeDtypeStruct((HALF, LINES_DEV), jnp.float32),
        compiler_params=pltpu.CompilerParams(vmem_limit_bytes=32 * 1024 * 1024),
        cost_estimate=pl.CostEstimate(
            flops=steps * 8 * HALF * LINES_DEV * SUB * 2,
            bytes_accessed=steps * LINES_DEV * SUB * 4,
            transcendentals=0,
        ),
        name="load_flow",
    )(idx, x, ptdf)


def slot_flow_kernel(idx_ref, x_ref, hi_ref, lo_ref, o_ref):
    @pl.when(pl.program_id(0) == 0)
    def _():
        o_ref[...] = jnp.zeros_like(o_ref)

    o_ref[...] += three_pass(lanes(x_ref, CAP), hi_ref[...], lo_ref[...], NT)


def slot_flow(x, w_hi, w_lo, idx):
    steps = idx.shape[0]
    return pl.pallas_call(
        slot_flow_kernel,
        grid_spec=pltpu.PrefetchScalarGridSpec(
            num_scalar_prefetch=1,
            grid=(steps,),
            in_specs=[
                pl.BlockSpec((SLOT_ROWS, 128), lambda i, idx: (i, 0)),
                pl.BlockSpec((LINES_DEV, SLOTS), lambda i, idx: (0, idx[i])),
                pl.BlockSpec((LINES_DEV, SLOTS), lambda i, idx: (0, idx[i])),
            ],
            out_specs=pl.BlockSpec((HALF, LINES_DEV), lambda i, idx: (0, 0)),
        ),
        out_shape=jax.ShapeDtypeStruct((HALF, LINES_DEV), jnp.float32),
        compiler_params=pltpu.CompilerParams(vmem_limit_bytes=32 * 1024 * 1024),
        cost_estimate=pl.CostEstimate(
            flops=steps * 8 * HALF * LINES_DEV * SLOTS * 2,
            bytes_accessed=steps * LINES_DEV * SLOTS * 4,
            transcendentals=0,
        ),
        name="slot_flow",
    )(idx, x, w_hi, w_lo)


def slot_price_kernel(idx_ref, x_ref, hi_ref, lo_ref, o_ref):
    p = three_pass(x_ref[...], hi_ref[...], lo_ref[...], NN)
    for r in range(CAP):
        o_ref[r * HALF : (r + 1) * HALF, :] = p[:, r * 128 : (r + 1) * 128]


def slot_price(x, w_hi, w_lo, idx):
    steps = idx.shape[0]
    return pl.pallas_call(
        slot_price_kernel,
        grid_spec=pltpu.PrefetchScalarGridSpec(
            num_scalar_prefetch=1,
            grid=(steps,),
            in_specs=[
                pl.BlockSpec((HALF, LINES_DEV), lambda i, idx: (0, 0)),
                pl.BlockSpec((LINES_DEV, SLOTS), lambda i, idx: (0, idx[i])),
                pl.BlockSpec((LINES_DEV, SLOTS), lambda i, idx: (0, idx[i])),
            ],
            out_specs=pl.BlockSpec((SLOT_ROWS, 128), lambda i, idx: (i, 0)),
        ),
        out_shape=jax.ShapeDtypeStruct((steps * SLOT_ROWS, 128), jnp.float32),
        compiler_params=pltpu.CompilerParams(vmem_limit_bytes=32 * 1024 * 1024),
        cost_estimate=pl.CostEstimate(
            flops=steps * 8 * HALF * LINES_DEV * SLOTS * 2,
            bytes_accessed=steps * LINES_DEV * SLOTS * 4,
            transcendentals=0,
        ),
        name="slot_price",
    )(idx, x, w_hi, w_lo)


def pick_kernel(idx_ref, code_ref, w_ref, hi_ref, lo_ref):
    w_hi, w_lo = split(w_ref[...])
    code = code_ref[0]
    code = jnp.concatenate([code[r : r + 1, :] for r in range(CAP)], axis=1)
    hot = lax.broadcasted_iota(jnp.int32, (SUB, SLOTS), 0).astype(jnp.float32) + 1.0 == code
    hot = hot.astype(jnp.float32).astype(jnp.bfloat16)
    picked = lax.dot_general(
        jnp.concatenate([w_hi, w_lo], axis=0), hot, NN, preferred_element_type=jnp.float32
    ).astype(jnp.bfloat16)
    hi_ref[...] = picked[:LINES_DEV]
    lo_ref[...] = picked[LINES_DEV:]


def pick(codes, ptdf, idx):
    return pl.pallas_call(
        pick_kernel,
        grid_spec=pltpu.PrefetchScalarGridSpec(
            num_scalar_prefetch=1,
            grid=(N_BAND,),
            in_specs=[
                pl.BlockSpec((1, CAP, 128), lambda i, idx: (idx[i], 0, 0)),
                pl.BlockSpec((LINES_DEV, SUB), lambda i, idx: (0, idx[i])),
            ],
            out_specs=[
                pl.BlockSpec((LINES_DEV, SLOTS), lambda i, idx: (0, i)),
                pl.BlockSpec((LINES_DEV, SLOTS), lambda i, idx: (0, i)),
            ],
        ),
        out_shape=[jax.ShapeDtypeStruct((LINES_DEV, N_BAND * SLOTS), jnp.bfloat16)] * 2,
        compiler_params=pltpu.CompilerParams(vmem_limit_bytes=32 * 1024 * 1024),
        cost_estimate=pl.CostEstimate(
            flops=N_BAND * 4 * LINES_DEV * SLOTS * SUB,
            bytes_accessed=N_BAND * LINES_DEV * (SUB + SLOTS) * 4,
            transcendentals=0,
        ),
        name="pick",
    )(idx, codes, ptdf)


def owner_slots(bus_map):
    block = bus_map // BUS_DEV
    within = bus_map % BUS_DEV
    owner = within // SUB * N_BUS + block
    local = within % SUB
    same = owner[:, None] == owner[None, :]
    earlier = lax.broadcasted_iota(jnp.int32, same.shape, 0) > lax.broadcasted_iota(
        jnp.int32, same.shape, 1
    )
    rank = jnp.sum((same & earlier).astype(jnp.int32), axis=1)
    return owner * CAP + rank, local


def on_device(
    dispatch0, cost_lin, cost_quad, gen_max, bus_map, demand, ptdf, line_price0, flow_max
):
    band = lax.axis_index("band")
    z, x, y = band // (NX * NY), band // NY % NX, band % NY
    rel = [(ry, rx, rz) for ry in range(NY) for rx in range(NX) for rz in range(NZ)]
    block_of = jnp.stack(
        [band_index((z + rz) % NZ, (x + rx) % NX, (y + ry) % NY) for ry, rx, rz in rel]
    ).astype(jnp.int32)
    place_a = [
        [ry * 8 + rx * 2 + rz for rx in range(NX) for rz in range(NZ)] for ry in range(NY)
    ]
    place_b = [
        [ry * 8 + rx * 2 + rz for ry in range(NY) for rz in range(NZ)] for rx in range(NX)
    ]
    place = (place_a, place_b)

    def const_idx(p):
        return jnp.array(p, jnp.int32)

    load = demand[:, 0, :].reshape(2, HALF, SUB // 128, 128)
    load = load.transpose(0, 2, 1, 3).reshape(2, LOAD_ROWS, 128)
    load_chunks = gather_band(load[0], load[1])

    target, local = owner_slots(bus_map)
    params = jnp.stack([(local + 1).astype(jnp.float32), cost_lin, cost_quad, gen_max], axis=1)
    total = DEVICES * CAP
    sent = jnp.zeros((total, S), jnp.float32).at[target].set(dispatch0.T)
    sent_params = jnp.zeros((total, 4), jnp.float32).at[target].set(params)
    sent = sent.reshape(DEVICES, CAP, 2, HALF).transpose(0, 2, 1, 3).reshape(DEVICES, CAP * S)
    codes = sent_params[:, 0].reshape(N_BAND, N_BUS, CAP).transpose(1, 0, 2)
    codes = jnp.broadcast_to(
        codes.reshape(1, N_BUS, N_BAND * CAP), (N_BAND, N_BUS, N_BAND * CAP)
    ).reshape(DEVICES, N_BAND * CAP)
    message = jnp.concatenate(
        [sent, sent_params.reshape(DEVICES, CAP * 4), codes], axis=1
    )
    got = lax.all_to_all(message, ("band", "bus"), split_axis=0, concat_axis=0, tiled=True).T
    slot_values = got[: CAP * S].reshape(2, CAP, HALF, 128)
    slot_params = got[CAP * S : CAP * S + CAP * 4].reshape(CAP, 4, 128)
    codes = got[CAP * S + CAP * 4 :].reshape(N_BAND, CAP, 128)
    lin = slot_params[None, :, 1:2]
    quad = slot_params[None, :, 2:3]
    top = slot_params[None, :, 3:4]

    w_hi, w_lo = pick(codes, ptdf, block_of)

    def slots_flow_of(values):
        rows = values.reshape(2, SLOT_ROWS, 128)
        chunks = gather_band(rows[0], rows[1])
        return [
            sum(
                slot_flow(chunks[k][r], w_hi, w_lo, const_idx(place[k][r])) for r in range(4)
            )
            for k in range(2)
        ]

    load_part = [
        sum(load_flow(load_chunks[k][r], ptdf, block_of[jnp.array(place[k][r])]) for r in range(4))
        for k in range(2)
    ]

    line_price = line_price0
    bound = dual_step * flow_max
    for iteration in range(ITERS):
        slot_part = slots_flow_of(slot_values)
        partial = jnp.concatenate(
            [slot_part[k] - load_part[k] for k in range(2)], axis=0
        )
        parts = lax.all_gather(partial, "bus", axis=0)
        flow = (parts[0] + parts[1]) + (parts[2] + parts[3])
        trial = line_price + dual_step * flow
        price_next = trial - jnp.clip(trial, -bound, bound)
        reflected = 2.0 * price_next - line_price
        line_price = price_next
        chunks = [
            [
                slot_price(
                    reflected[k * HALF : (k + 1) * HALF], w_hi, w_lo, const_idx(place[k][r])
                )
                for r in range(4)
            ]
            for k in range(2)
        ]
        price_a, price_b = sum_band(*chunks)
        unit = jnp.stack([price_a, price_b]).reshape(2, CAP, HALF, 128)
        slot_values = jnp.clip(
            (slot_values - primal_step * (lin + unit)) / (1.0 + primal_step * quad), 0.0, top
        )
    home = lax.all_to_all(
        slot_values.reshape(CAP * S, 128).T, ("band", "bus"), split_axis=0, concat_axis=0, tiled=True
    )
    home = home.reshape(DEVICES, 2, CAP, HALF).transpose(0, 2, 1, 3).reshape(total, S)
    return home[target].T, line_price


def solution(mesh):
    gens = P(("band", "bus"))
    in_specs = (
        P(None, ("band", "bus")),
        gens,
        gens,
        gens,
        gens,
        P(None, "bus", "band"),
        P("band", "bus"),
        P(None, "band"),
        P("band"),
    )
    out_specs = (P(None, ("band", "bus")), P(None, "band"))
    return jax.shard_map(
        on_device, mesh=mesh, in_specs=in_specs, out_specs=out_specs, check_vma=False
    )
```

```python
import jax
import jax.numpy as jnp
from jax import lax
from jax.experimental import pallas as pl
from jax.experimental.pallas import tpu as pltpu
from jax.sharding import PartitionSpec as P

ITERS = 2
S = 64
SUB = 768
CAP = 3
N_BUS = 4
N_BAND = 32
SLOTS = CAP * 128
LINES_DEV = 256
LOAD_ROWS = SUB // 128 * S
SLOT_ROWS = CAP * S

primal_step = 0.5
dual_step = 1.0

NZ, NX, NY = 2, 4, 4
NT = (((1,), (1,)), ((), ()))
NN = (((1,), (0,)), ((), ()))
VMEM = 48 * 1024 * 1024


def band_index(z, x, y):
    return (z * NX + x) * NY + y


def steps_of(stage, core, r):
    if stage == "z":
        return (r, 0, 0)
    along_x = (stage == "first") == (core == 0)
    return (0, r, 0) if along_x else (0, 0, r)


def moved(a, stage, r):
    pairs = []
    for z in range(NZ):
        for x in range(NX):
            for y in range(NY):
                for j in range(N_BUS):
                    dz, dx, dy = steps_of(stage, j % 2, r)
                    to = band_index((z + dz) % NZ, (x + dx) % NX, (y + dy) % NY)
                    pairs.append((band_index(z, x, y) * N_BUS + j, to * N_BUS + j))
    return lax.ppermute(a, ("band", "bus"), pairs)


def gather_z(block):
    return jnp.concatenate([block, moved(block, "z", 1)], axis=0)


def gather_second(eight):
    one, three, two = (moved(eight, "second", -r) for r in (1, 3, 2))
    return [eight, one, two, three]


def ring_first(pair):
    one, three, two = (moved(pair, "first", -r) for r in (1, 3, 2))
    return pair, one, two, three


def gather_first(pair):
    return jnp.concatenate(ring_first(pair), axis=0)


def gather_second(eight):
    one, three, two = (moved(eight, "second", -r) for r in (1, 3, 2))
    return [eight, one, two, three]


def sum_bus(a):
    got = [
        lax.ppermute(a, "bus", [(j, j ^ k) for j in range(N_BUS)]) for k in (2, 3, 1)
    ]
    return (a + got[2]) + (got[0] + got[1])


def sum_band(chunks):
    got = [moved(chunks[r], "second", r) for r in (2, 1, 3)]
    eight = chunks[0] + got[0] + got[1] + got[2]
    n = eight.shape[0] // 4
    parts = [eight[r * n : (r + 1) * n] for r in range(4)]
    got = [moved(parts[r], "first", r) for r in (2, 1, 3)]
    return parts[0] + got[0] + got[1] + got[2]


def sum_z(pair, both):
    n = pair.shape[0] // 2
    if both:
        got = moved(pair, "z", 1)
        return pair + jnp.concatenate([got[n:], got[:n]], axis=0)
    return pair[:n] + moved(pair[n:], "z", 1)


def split(v):
    hi = v.astype(jnp.bfloat16)
    lo = (v - hi.astype(jnp.float32)).astype(jnp.bfloat16)
    return hi, lo


def three_pass(x, w, dims):
    x_hi, x_lo = split(x)
    w_hi, w_lo = split(w)
    n = x.shape[0]
    y = lax.dot_general(
        jnp.concatenate([x_hi, x_lo], axis=0), w_hi, dims, preferred_element_type=jnp.float32
    )
    return y[:n] + (
        y[n:] + lax.dot_general(x_hi, w_lo, dims, preferred_element_type=jnp.float32)
    )


def lanes(ref, count):
    n = ref.shape[0] // count
    return jnp.concatenate([ref[k * n : (k + 1) * n, :] for k in range(count)], axis=1)


def cost(us):
    return pl.CostEstimate(flops=0, bytes_accessed=int(us * 3.0e6), transcendentals=0)


BLOCK_ROWS = LOAD_ROWS + SLOT_ROWS
FIRST_STEP = 4


def first_flow_kernel(idx_ref, load_acc_ref, slot_acc_ref, x_ref, columns_ref, *refs):
    *w_refs, load_ref, slot_ref = refs

    @pl.when(pl.program_id(0) == 0)
    def _():
        load_ref[...] = load_acc_ref[...]
        slot_ref[...] = slot_acc_ref[...]

    load, slots = [], []
    for u in range(0, FIRST_STEP, NZ):
        base = u * BLOCK_ROWS
        load += [x_ref[base + k * S : base + (k + 1) * S, :] for k in range(NZ * SUB // 128)]
        base += NZ * LOAD_ROWS
        slots += [x_ref[base + k * S : base + (k + 1) * S, :] for k in range(NZ * CAP)]
    w = jnp.concatenate([ref[...] for ref in w_refs], axis=1)
    columns = columns_ref[...].reshape(FIRST_STEP * SLOTS, LINES_DEV)
    load_ref[...] -= three_pass(jnp.concatenate(load, axis=1), w, NT)
    slot_ref[...] += three_pass(jnp.concatenate(slots, axis=1), columns, NN)


def first_flow(load_acc, slot_acc, x, columns, ptdf, block_of, start):
    steps = x.shape[0] // (FIRST_STEP * BLOCK_ROWS)
    at = start // FIRST_STEP

    def sub(u):
        return pl.BlockSpec(
            (LINES_DEV, SUB), lambda i, idx: (0, idx[start + i * FIRST_STEP + u])
        )

    return pl.pallas_call(
        first_flow_kernel,
        grid_spec=pltpu.PrefetchScalarGridSpec(
            num_scalar_prefetch=1,
            grid=(steps,),
            in_specs=[
                pl.BlockSpec((S, LINES_DEV), lambda i, idx: (0, 0)),
                pl.BlockSpec((S, LINES_DEV), lambda i, idx: (0, 0)),
                pl.BlockSpec((FIRST_STEP * BLOCK_ROWS, 128), lambda i, idx: (i, 0)),
                pl.BlockSpec((FIRST_STEP, SLOTS, LINES_DEV), lambda i, idx: (at + i, 0, 0)),
            ]
            + [sub(u) for u in range(FIRST_STEP)],
            out_specs=[pl.BlockSpec((S, LINES_DEV), lambda i, idx: (0, 0))] * 2,
        ),
        out_shape=[jax.ShapeDtypeStruct((S, LINES_DEV), jnp.float32)] * 2,
        compiler_params=pltpu.CompilerParams(vmem_limit_bytes=VMEM),
        cost_estimate=cost(3.0 * steps),
        name="first_flow",
    )(block_of, load_acc, slot_acc, x, columns, *([ptdf] * FIRST_STEP))


SLOT_STEPS = 2
SLOT_STEP = 8 // SLOT_STEPS


def slot_flow_kernel(acc_ref, x_ref, w_ref, o_ref):
    @pl.when(pl.program_id(0) == 0)
    def _():
        o_ref[...] = acc_ref[...]

    w = w_ref[...].reshape(SLOT_STEP * SLOTS, LINES_DEV)
    o_ref[...] += three_pass(lanes(x_ref, SLOT_STEP * CAP), w, NN)


def slot_flow(acc, x, columns, r2):
    s = acc.shape[0]
    return pl.pallas_call(
        slot_flow_kernel,
        grid=(SLOT_STEPS,),
        in_specs=[
            pl.BlockSpec((s, LINES_DEV), lambda i: (0, 0)),
            pl.BlockSpec((SLOT_STEP * CAP * s, 128), lambda i: (i, 0)),
            pl.BlockSpec(
                (SLOT_STEP, SLOTS, LINES_DEV), lambda i: (r2 * SLOT_STEPS + i, 0, 0)
            ),
        ],
        out_specs=pl.BlockSpec((s, LINES_DEV), lambda i: (0, 0)),
        out_shape=jax.ShapeDtypeStruct((s, LINES_DEV), jnp.float32),
        compiler_params=pltpu.CompilerParams(vmem_limit_bytes=VMEM),
        cost_estimate=cost(2.0),
        name="slot_flow",
    )(acc, x, columns)


def slot_price_kernel(x_ref, w_ref, *o_refs):
    w = w_ref[...].reshape(8 * SLOTS, LINES_DEV)
    p = three_pass(x_ref[...], w, NT)
    for step, o_ref in enumerate(o_refs):

        @pl.when(pl.program_id(0) == step)
        def _():
            for k in range(8 * CAP):
                o_ref[k * S : (k + 1) * S, :] = p[:, k * 128 : (k + 1) * 128]


def slot_price(x, columns, chunks):
    n, top = len(chunks), chunks[0]
    return pl.pallas_call(
        slot_price_kernel,
        grid=(n,),
        in_specs=[
            pl.BlockSpec((S, LINES_DEV), lambda i: (0, 0)),
            pl.BlockSpec((8, SLOTS, LINES_DEV), lambda i: (top - i, 0, 0)),
        ],
        out_specs=[pl.BlockSpec((8 * SLOT_ROWS, 128), lambda i: (0, 0))] * n,
        out_shape=[jax.ShapeDtypeStruct((8 * SLOT_ROWS, 128), jnp.float32)] * n,
        compiler_params=pltpu.CompilerParams(vmem_limit_bytes=VMEM),
        cost_estimate=cost(2.0 * n),
        name="slot_price",
    )(x, columns)


PICK_STEP = 4
HOT = CAP * N_BUS


def pick_kernel(code_ref, w_ref, o_ref):
    codes = code_ref[...]
    column = lax.broadcasted_iota(jnp.int32, codes.shape, 1)
    bus = lax.broadcasted_iota(jnp.int32, (SLOTS, SUB), 1).astype(jnp.float32) + 1.0
    for u in range(PICK_STEP):
        i = pl.program_id(0) * PICK_STEP + u
        w_hi, w_lo = split(w_ref[:, u * SUB : (u + 1) * SUB])
        code = jnp.sum(jnp.where(column == i, codes, 0.0), axis=1, keepdims=True)
        hot = (bus == code).astype(jnp.float32).astype(jnp.bfloat16)
        picked = lax.dot_general(hot, w_hi, NT, preferred_element_type=jnp.float32)
        picked += lax.dot_general(hot, w_lo, NT, preferred_element_type=jnp.float32)
        for b in range(N_BAND):
            for q in range(HOT):
                o_ref[b, pl.ds(q * N_BAND + i, 1), :] = picked[b * HOT + q : b * HOT + q + 1, :]


def pick(codes, ptdf):
    return pl.pallas_call(
        pick_kernel,
        grid=(N_BAND // PICK_STEP,),
        in_specs=[
            pl.BlockSpec((SLOTS, N_BAND), lambda i: (0, 0)),
            pl.BlockSpec((LINES_DEV, PICK_STEP * SUB), lambda i: (0, i)),
        ],
        out_specs=pl.BlockSpec((N_BAND, SLOTS, LINES_DEV), lambda i: (0, 0, 0)),
        out_shape=jax.ShapeDtypeStruct((N_BAND, SLOTS, LINES_DEV), jnp.float32),
        compiler_params=pltpu.CompilerParams(vmem_limit_bytes=VMEM),
        cost_estimate=cost(30.0),
        name="pick",
    )(codes, ptdf)


def home_columns(bus_map):
    owner = bus_map // SUB
    same = owner[:, None] == owner[None, :]
    earlier = lax.broadcasted_iota(jnp.int32, same.shape, 0) > lax.broadcasted_iota(
        jnp.int32, same.shape, 1
    )
    rank = jnp.sum((same & earlier).astype(jnp.int32), axis=1)
    return owner // N_BAND * 128 + rank * N_BAND + owner % N_BAND, bus_map % SUB


def exact_dot(a, b, dims):
    return lax.dot_general(
        a, b, dims, precision=lax.Precision.HIGHEST, preferred_element_type=jnp.float32
    )


def on_device(
    dispatch0, cost_lin, cost_quad, gen_max, bus_map, demand, ptdf, line_price0, flow_max
):
    band = lax.axis_index("band")
    core = lax.axis_index("bus") % 2
    z, x, y = band // (NX * NY), band // NY % NX, band % NY
    rel = lax.iota(jnp.int32, N_BAND)
    r2, r1, rz = rel // 8, rel // 2 % 4, rel % 2
    dx, dy = jnp.where(core == 0, r1, r2), jnp.where(core == 0, r2, r1)
    block_of = band_index((z + rz) % NZ, (x + dx) % NX, (y + dy) % NY)

    at, local = home_columns(bus_map)
    where = (at[:, None] == lax.broadcasted_iota(jnp.int32, (1, N_BUS * 128), 1)).astype(
        jnp.float32
    )
    own = jnp.concatenate(
        [
            dispatch0,
            (local + 1).astype(jnp.float32)[None],
            cost_lin[None],
            cost_quad[None],
            gen_max[None],
            jnp.zeros((4, dispatch0.shape[1]), jnp.float32),
        ],
        axis=0,
    )
    rows = own.shape[0]
    message = exact_dot(own, where, NN).reshape(rows, N_BUS, 128).transpose(1, 0, 2)
    message_got = lax.all_to_all(message, "bus", split_axis=0, concat_axis=0, tiled=True)
    got = message_got
    got = got[:, :, : CAP * N_BAND].reshape(N_BUS, rows, CAP, N_BAND)
    got = got.transpose(2, 1, 0, 3).reshape(CAP, rows, 128)
    load = demand[:, 0, :].reshape(S, SUB // 128, 128).transpose(1, 0, 2)
    load = gather_z(load.reshape(LOAD_ROWS, 128))
    codes = jnp.pad(got[:, S], ((0, 8 - CAP), (0, 0)))
    codes = lax.all_to_all(
        jnp.broadcast_to(codes, (N_BAND, 8, 128)), "band", split_axis=0, concat_axis=0, tiled=True
    )
    codes = codes[:, :CAP][block_of].reshape(SLOTS, N_BAND)
    params = jnp.pad(
        got[:, S + 1 : S + 4].transpose(1, 0, 2).reshape(3 * CAP, 128), ((0, 16 - 3 * CAP), (0, 0))
    )
    slots = gather_z(
        jnp.concatenate([got[:, :S].reshape(SLOT_ROWS, 128), params], axis=0)
    ).reshape(2, SLOT_ROWS + 16, 128)
    params = slots[:, SLOT_ROWS : SLOT_ROWS + 3 * CAP].reshape(2, 3, CAP, 1, 128)
    lin, quad, top = (params[:, k] for k in range(3))
    slots = slots[:, :SLOT_ROWS].reshape(2 * SLOT_ROWS, 128)
    now = slots.reshape(2, CAP, S, 128)
    load, _ = lax.optimization_barrier((load, message_got))
    parts = []
    for at in zip(ring_first(load), ring_first(slots)):
        parts += at
    eight = jnp.concatenate(parts, axis=0)
    eight, codes = lax.optimization_barrier((eight, codes))
    columns = pick(codes, ptdf)
    one, three = moved(eight, "second", -1), moved(eight, "second", -3)
    one, three, columns = lax.optimization_barrier((one, three, columns))
    n = eight.shape[0] // 2
    two_near, two_far = moved(one[:n], "second", -1), moved(three[n:], "second", -3)
    load_part = slot_part = jnp.zeros((S, LINES_DEV), jnp.float32)
    for x, at in ((eight, 0), (one, 8), (three, 24), (two_near, 16), (two_far, 20)):
        load_part, slot_part = first_flow(
            load_part, slot_part, x, columns, ptdf, block_of, at
        )
    flow = load_part + slot_part

    bound = dual_step * flow_max
    line_price = line_price0
    for iteration in range(ITERS):
        last = iteration == ITERS - 1
        trial = line_price + dual_step * sum_bus(flow)
        price_next = trial - jnp.clip(trial, -bound, bound)
        reflected = 2.0 * price_next - line_price
        line_price = price_next
        three, two, one = slot_price(reflected, columns, (3, 2, 1))
        chunks = [*slot_price(reflected, columns, (0,)), one, two, three]
        unit = sum_z(sum_band(chunks), not last)
        unit = unit.reshape(-1, CAP, S, 128)
        k = unit.shape[0]
        before = now[:k]
        now = jnp.clip(
            (before - primal_step * (lin[:k] + unit)) / (1.0 + primal_step * quad[:k]),
            0.0,
            top[:k],
        )
        if not last:
            slots = gather_second(gather_first(now.reshape(2 * SLOT_ROWS, 128)))
            flow = load_part
            for r in (0, 1, 3, 2):
                flow = slot_flow(flow, slots[r], columns, r)
    slot_values = now[0]
    home = slot_values.reshape(CAP, S, N_BUS, N_BAND).transpose(2, 1, 0, 3)
    home = home.reshape(N_BUS, S, CAP * N_BAND)
    home = jnp.pad(home, ((0, 0), (0, 0), (0, 128 - CAP * N_BAND)))
    home = lax.all_to_all(home, "bus", split_axis=0, concat_axis=0, tiled=True)
    dispatch = exact_dot(home.transpose(1, 0, 2).reshape(S, N_BUS * 128), where, NT)
    return dispatch, line_price


def solution(mesh):
    gens = P(("band", "bus"))
    in_specs = (
        P(None, ("band", "bus")),
        gens,
        gens,
        gens,
        gens,
        P(None, "bus", "band"),
        P("band", "bus"),
        P(None, "band"),
        P("band"),
    )
    out_specs = (P(None, ("band", "bus")), P(None, "band"))
    return jax.shard_map(
        on_device, mesh=mesh, in_specs=in_specs, out_specs=out_specs, check_vma=False
    )
```

```python
import functools

import jax
import jax.numpy as jnp
from jax import lax
from jax.experimental import pallas as pl
from jax.experimental.pallas import tpu as pltpu
from jax.sharding import PartitionSpec as P

ITERS = 2
S = 64
SUB = 768
CAP = 3
N_BUS = 4
N_BAND = 32
SLOTS = CAP * 128
LINES_DEV = 256
LOAD_ROWS = SUB // 128 * S
SLOT_ROWS = CAP * S

primal_step = 0.5
dual_step = 1.0

NZ, NX, NY = 2, 4, 4
NT = (((1,), (1,)), ((), ()))
NN = (((1,), (0,)), ((), ()))
VMEM = 48 * 1024 * 1024


def band_index(z, x, y):
    return (z * NX + x) * NY + y


def steps_of(stage, core, r):
    if stage == "z":
        return (r, 0, 0)
    along_x = (stage == "first") == (core == 0)
    return (0, r, 0) if along_x else (0, 0, r)


def moved(a, stage, r):
    pairs = []
    for z in range(NZ):
        for x in range(NX):
            for y in range(NY):
                for j in range(N_BUS):
                    dz, dx, dy = steps_of(stage, j % 2, r)
                    to = band_index((z + dz) % NZ, (x + dx) % NX, (y + dy) % NY)
                    pairs.append((band_index(z, x, y) * N_BUS + j, to * N_BUS + j))
    return lax.ppermute(a, ("band", "bus"), pairs)


def gather_z(block):
    return jnp.concatenate([block, moved(block, "z", 1)], axis=0)


def gather_second(eight):
    one, three, two = (moved(eight, "second", -r) for r in (1, 3, 2))
    return [eight, one, two, three]


def ring_first(pair):
    one, three, two = (moved(pair, "first", -r) for r in (1, 3, 2))
    return pair, one, two, three


def gather_first(pair):
    return jnp.concatenate(ring_first(pair), axis=0)


def gather_second(eight):
    one, three, two = (moved(eight, "second", -r) for r in (1, 3, 2))
    return [eight, one, two, three]


def sum_bus(a):
    got = [
        lax.ppermute(a, "bus", [(j, j ^ k) for j in range(N_BUS)]) for k in (2, 3, 1)
    ]
    return (a + got[2]) + (got[0] + got[1])


def sum_band(chunks):
    got = [moved(chunks[r], "second", r) for r in (2, 1, 3)]
    eight = chunks[0] + got[0] + got[1] + got[2]
    n = eight.shape[0] // 4
    parts = [eight[r * n : (r + 1) * n] for r in range(4)]
    got = [moved(parts[r], "first", r) for r in (2, 1, 3)]
    return parts[0] + got[0] + got[1] + got[2]


def sum_z(pair, both):
    n = pair.shape[0] // 2
    if both:
        got = moved(pair, "z", 1)
        return pair + jnp.concatenate([got[n:], got[:n]], axis=0)
    return pair[:n] + moved(pair[n:], "z", 1)


def split(v):
    hi = v.astype(jnp.bfloat16)
    lo = (v - hi.astype(jnp.float32)).astype(jnp.bfloat16)
    return hi, lo


def three_pass(x, w, dims):
    x_hi, x_lo = split(x)
    w_hi, w_lo = split(w)
    n = x.shape[0]
    y = lax.dot_general(
        jnp.concatenate([x_hi, x_lo], axis=0), w_hi, dims, preferred_element_type=jnp.float32
    )
    return y[:n] + (
        y[n:] + lax.dot_general(x_hi, w_lo, dims, preferred_element_type=jnp.float32)
    )


def lanes(ref, count):
    n = ref.shape[0] // count
    return jnp.concatenate([ref[k * n : (k + 1) * n, :] for k in range(count)], axis=1)


def cost(us):
    return pl.CostEstimate(flops=0, bytes_accessed=int(us * 3.0e6), transcendentals=0)


BLOCK_ROWS = LOAD_ROWS + SLOT_ROWS
FIRST_STEP = 4


def first_flow_kernel(steps, idx_ref, at_ref, load_acc_ref, slot_acc_ref, columns_ref, *refs):
    *refs, load_ref, slot_ref = refs
    w_refs, x_refs = refs[:FIRST_STEP], refs[FIRST_STEP:]
    i = pl.program_id(0)

    @pl.when(i == 0)
    def _():
        load_ref[...] = load_acc_ref[...]
        slot_ref[...] = slot_acc_ref[...]

    def add(x_ref):
        load, slots = [], []
        for u in range(0, FIRST_STEP, NZ):
            base = u * BLOCK_ROWS
            load += [x_ref[base + k * S : base + (k + 1) * S, :] for k in range(NZ * SUB // 128)]
            base += NZ * LOAD_ROWS
            slots += [x_ref[base + k * S : base + (k + 1) * S, :] for k in range(NZ * CAP)]
        w = jnp.concatenate([ref[...] for ref in w_refs], axis=1)
        columns = columns_ref[...].reshape(FIRST_STEP * SLOTS, LINES_DEV)
        load_ref[...] -= three_pass(jnp.concatenate(load, axis=1), w, NT)
        slot_ref[...] += three_pass(jnp.concatenate(slots, axis=1), columns, NN)

    for k, x_ref in enumerate(x_refs):
        pl.when(i // steps == k)(lambda x_ref=x_ref: add(x_ref))


def first_flow(load_acc, slot_acc, xs, columns, ptdf, block_of, starts):
    steps = xs[0].shape[0] // (FIRST_STEP * BLOCK_ROWS)
    places = [start // FIRST_STEP + i for start in starts for i in range(steps)]
    order = jnp.concatenate(
        [block_of[start : start + steps * FIRST_STEP] for start in starts]
    )

    def sub(u):
        return pl.BlockSpec((LINES_DEV, SUB), lambda i, idx, at: (0, idx[i * FIRST_STEP + u]))

    def piece(k):
        return pl.BlockSpec(
            (FIRST_STEP * BLOCK_ROWS, 128),
            lambda i, idx, at: (jnp.clip(i - k * steps, 0, steps - 1), 0),
        )

    whole = pl.BlockSpec((S, LINES_DEV), lambda i, idx, at: (0, 0))
    return pl.pallas_call(
        functools.partial(first_flow_kernel, steps),
        grid_spec=pltpu.PrefetchScalarGridSpec(
            num_scalar_prefetch=2,
            grid=(len(places),),
            in_specs=[
                whole,
                whole,
                pl.BlockSpec((FIRST_STEP, SLOTS, LINES_DEV), lambda i, idx, at: (at[i], 0, 0)),
            ]
            + [sub(u) for u in range(FIRST_STEP)]
            + [piece(k) for k in range(len(xs))],
            out_specs=[whole] * 2,
        ),
        out_shape=[jax.ShapeDtypeStruct((S, LINES_DEV), jnp.float32)] * 2,
        compiler_params=pltpu.CompilerParams(vmem_limit_bytes=VMEM),
        cost_estimate=cost(3.0 * len(places)),
        name="first_flow",
    )(
        order,
        jnp.array(places, jnp.int32),
        load_acc,
        slot_acc,
        columns,
        *([ptdf] * FIRST_STEP),
        *xs,
    )


SLOT_STEPS = 2
SLOT_STEP = 8 // SLOT_STEPS


def slot_flow_kernel(acc_ref, x_ref, w_ref, o_ref):
    @pl.when(pl.program_id(0) == 0)
    def _():
        o_ref[...] = acc_ref[...]

    w = w_ref[...].reshape(SLOT_STEP * SLOTS, LINES_DEV)
    o_ref[...] += three_pass(lanes(x_ref, SLOT_STEP * CAP), w, NN)


def slot_flow(acc, x, columns, r2):
    s = acc.shape[0]
    return pl.pallas_call(
        slot_flow_kernel,
        grid=(SLOT_STEPS,),
        in_specs=[
            pl.BlockSpec((s, LINES_DEV), lambda i: (0, 0)),
            pl.BlockSpec((SLOT_STEP * CAP * s, 128), lambda i: (i, 0)),
            pl.BlockSpec(
                (SLOT_STEP, SLOTS, LINES_DEV), lambda i: (r2 * SLOT_STEPS + i, 0, 0)
            ),
        ],
        out_specs=pl.BlockSpec((s, LINES_DEV), lambda i: (0, 0)),
        out_shape=jax.ShapeDtypeStruct((s, LINES_DEV), jnp.float32),
        compiler_params=pltpu.CompilerParams(vmem_limit_bytes=VMEM),
        cost_estimate=cost(2.0),
        name="slot_flow",
    )(acc, x, columns)


def slot_price_kernel(x_ref, w_ref, *o_refs):
    w = w_ref[...].reshape(8 * SLOTS, LINES_DEV)
    p = three_pass(x_ref[...], w, NT)
    for step, o_ref in enumerate(o_refs):

        @pl.when(pl.program_id(0) == step)
        def _():
            for k in range(8 * CAP):
                o_ref[k * S : (k + 1) * S, :] = p[:, k * 128 : (k + 1) * 128]


def slot_price(x, columns, chunks):
    n, top = len(chunks), chunks[0]
    return pl.pallas_call(
        slot_price_kernel,
        grid=(n,),
        in_specs=[
            pl.BlockSpec((S, LINES_DEV), lambda i: (0, 0)),
            pl.BlockSpec((8, SLOTS, LINES_DEV), lambda i: (top - i, 0, 0)),
        ],
        out_specs=[pl.BlockSpec((8 * SLOT_ROWS, 128), lambda i: (0, 0))] * n,
        out_shape=[jax.ShapeDtypeStruct((8 * SLOT_ROWS, 128), jnp.float32)] * n,
        compiler_params=pltpu.CompilerParams(vmem_limit_bytes=VMEM),
        cost_estimate=cost(2.0 * n),
        name="slot_price",
    )(x, columns)


PICK_STEP = 4
HOT = CAP * N_BUS


def pick_kernel(code_ref, w_ref, o_ref):
    codes = code_ref[...]
    column = lax.broadcasted_iota(jnp.int32, codes.shape, 1)
    bus = lax.broadcasted_iota(jnp.int32, (SLOTS, SUB), 1).astype(jnp.float32) + 1.0
    for u in range(PICK_STEP):
        i = pl.program_id(0) * PICK_STEP + u
        w_hi, w_lo = split(w_ref[:, u * SUB : (u + 1) * SUB])
        code = jnp.sum(jnp.where(column == i, codes, 0.0), axis=1, keepdims=True)
        hot = (bus == code).astype(jnp.float32).astype(jnp.bfloat16)
        picked = lax.dot_general(hot, w_hi, NT, preferred_element_type=jnp.float32)
        picked += lax.dot_general(hot, w_lo, NT, preferred_element_type=jnp.float32)
        for b in range(N_BAND):
            for q in range(HOT):
                o_ref[b, pl.ds(q * N_BAND + i, 1), :] = picked[b * HOT + q : b * HOT + q + 1, :]


def pick(codes, ptdf):
    return pl.pallas_call(
        pick_kernel,
        grid=(N_BAND // PICK_STEP,),
        in_specs=[
            pl.BlockSpec((SLOTS, N_BAND), lambda i: (0, 0)),
            pl.BlockSpec((LINES_DEV, PICK_STEP * SUB), lambda i: (0, i)),
        ],
        out_specs=pl.BlockSpec((N_BAND, SLOTS, LINES_DEV), lambda i: (0, 0, 0)),
        out_shape=jax.ShapeDtypeStruct((N_BAND, SLOTS, LINES_DEV), jnp.float32),
        compiler_params=pltpu.CompilerParams(vmem_limit_bytes=VMEM),
        cost_estimate=cost(30.0),
        name="pick",
    )(codes, ptdf)


def home_columns(bus_map):
    owner = bus_map // SUB
    same = owner[:, None] == owner[None, :]
    earlier = lax.broadcasted_iota(jnp.int32, same.shape, 0) > lax.broadcasted_iota(
        jnp.int32, same.shape, 1
    )
    rank = jnp.sum((same & earlier).astype(jnp.int32), axis=1)
    return owner // N_BAND * 128 + rank * N_BAND + owner % N_BAND, bus_map % SUB


def exact_dot(a, b, dims):
    return lax.dot_general(
        a, b, dims, precision=lax.Precision.HIGHEST, preferred_element_type=jnp.float32
    )


def on_device(
    dispatch0, cost_lin, cost_quad, gen_max, bus_map, demand, ptdf, line_price0, flow_max
):
    band = lax.axis_index("band")
    core = lax.axis_index("bus") % 2
    z, x, y = band // (NX * NY), band // NY % NX, band % NY
    rel = lax.iota(jnp.int32, N_BAND)
    r2, r1, rz = rel // 8, rel // 2 % 4, rel % 2
    dx, dy = jnp.where(core == 0, r1, r2), jnp.where(core == 0, r2, r1)
    block_of = band_index((z + rz) % NZ, (x + dx) % NX, (y + dy) % NY)

    at, local = home_columns(bus_map)
    where = (at[:, None] == lax.broadcasted_iota(jnp.int32, (1, N_BUS * 128), 1)).astype(
        jnp.float32
    )
    own = jnp.concatenate(
        [
            dispatch0,
            (local + 1).astype(jnp.float32)[None],
            cost_lin[None],
            cost_quad[None],
            gen_max[None],
            jnp.zeros((4, dispatch0.shape[1]), jnp.float32),
        ],
        axis=0,
    )
    rows = own.shape[0]
    message = exact_dot(own, where, NN).reshape(rows, N_BUS, 128).transpose(1, 0, 2)
    message_got = lax.all_to_all(message, "bus", split_axis=0, concat_axis=0, tiled=True)
    got = message_got
    got = got[:, :, : CAP * N_BAND].reshape(N_BUS, rows, CAP, N_BAND)
    got = got.transpose(2, 1, 0, 3).reshape(CAP, rows, 128)
    load = demand[:, 0, :].reshape(S, SUB // 128, 128).transpose(1, 0, 2)
    load = gather_z(load.reshape(LOAD_ROWS, 128))
    codes = jnp.pad(got[:, S], ((0, 8 - CAP), (0, 0)))
    codes, load = lax.optimization_barrier((codes, load))
    codes = lax.all_to_all(
        jnp.broadcast_to(codes, (N_BAND, 8, 128)), "band", split_axis=0, concat_axis=0, tiled=True
    )
    codes = codes[:, :CAP][block_of].reshape(SLOTS, N_BAND)
    params = jnp.pad(
        got[:, S + 1 : S + 4].transpose(1, 0, 2).reshape(3 * CAP, 128), ((0, 16 - 3 * CAP), (0, 0))
    )
    slots = gather_z(
        jnp.concatenate([got[:, :S].reshape(SLOT_ROWS, 128), params], axis=0)
    ).reshape(2, SLOT_ROWS + 16, 128)
    params = slots[:, SLOT_ROWS : SLOT_ROWS + 3 * CAP].reshape(2, 3, CAP, 1, 128)
    lin, quad, top = (params[:, k] for k in range(3))
    slots = slots[:, :SLOT_ROWS].reshape(2 * SLOT_ROWS, 128)
    now = slots.reshape(2, CAP, S, 128)
    load, _ = lax.optimization_barrier((load, message_got))
    parts = []
    for at in zip(ring_first(load), ring_first(slots)):
        parts += at
    eight = jnp.concatenate(parts, axis=0)
    eight, codes = lax.optimization_barrier((eight, codes))
    columns = pick(codes, ptdf)
    one, three = moved(eight, "second", -1), moved(eight, "second", -3)
    one, three, columns = lax.optimization_barrier((one, three, columns))
    n = eight.shape[0] // 2
    two_near, two_far = moved(one[:n], "second", -1), moved(three[n:], "second", -3)
    load_part = slot_part = jnp.zeros((S, LINES_DEV), jnp.float32)
    for xs, starts in (((eight, one, three), (0, 8, 24)), ((two_near, two_far), (16, 20))):
        load_part, slot_part = first_flow(
            load_part, slot_part, xs, columns, ptdf, block_of, starts
        )
    flow = load_part + slot_part

    bound = dual_step * flow_max
    line_price = line_price0
    for iteration in range(ITERS):
        last = iteration == ITERS - 1
        trial = line_price + dual_step * sum_bus(flow)
        price_next = trial - jnp.clip(trial, -bound, bound)
        reflected = 2.0 * price_next - line_price
        line_price = price_next
        three, two, one = slot_price(reflected, columns, (3, 2, 1))
        chunks = [*slot_price(reflected, columns, (0,)), one, two, three]
        unit = sum_z(sum_band(chunks), not last)
        unit = unit.reshape(-1, CAP, S, 128)
        k = unit.shape[0]
        before = now[:k]
        now = jnp.clip(
            (before - primal_step * (lin[:k] + unit)) / (1.0 + primal_step * quad[:k]),
            0.0,
            top[:k],
        )
        if not last:
            slots = gather_second(gather_first(now.reshape(2 * SLOT_ROWS, 128)))
            flow = load_part
            for r in (0, 1, 3, 2):
                flow = slot_flow(flow, slots[r], columns, r)
    slot_values = now[0]
    home = slot_values.reshape(CAP, S, N_BUS, N_BAND).transpose(2, 1, 0, 3)
    home = home.reshape(N_BUS, S, CAP * N_BAND)
    home = jnp.pad(home, ((0, 0), (0, 0), (0, 128 - CAP * N_BAND)))
    home = lax.all_to_all(home, "bus", split_axis=0, concat_axis=0, tiled=True)
    dispatch = exact_dot(home.transpose(1, 0, 2).reshape(S, N_BUS * 128), where, NT)
    return dispatch, line_price


def solution(mesh):
    gens = P(("band", "bus"))
    in_specs = (
        P(None, ("band", "bus")),
        gens,
        gens,
        gens,
        gens,
        P(None, "bus", "band"),
        P("band", "bus"),
        P(None, "band"),
        P("band"),
    )
    out_specs = (P(None, ("band", "bus")), P(None, "band"))
    return jax.shard_map(
        on_device, mesh=mesh, in_specs=in_specs, out_specs=out_specs, check_vma=False
    )
```

```python
import functools

import jax
import jax.numpy as jnp
from jax import lax
from jax.experimental import pallas as pl
from jax.experimental.pallas import tpu as pltpu
from jax.sharding import PartitionSpec as P

ITERS = 2
S = 64
SUB = 768
CAP = 3
N_BUS = 4
N_BAND = 32
SLOTS = CAP * 128
LINES_DEV = 256
LOAD_ROWS = SUB // 128 * S
SLOT_ROWS = CAP * S

primal_step = 0.5
dual_step = 1.0

NZ, NX, NY = 2, 4, 4
NT = (((1,), (1,)), ((), ()))
NN = (((1,), (0,)), ((), ()))
VMEM = 48 * 1024 * 1024


def band_index(z, x, y):
    return (z * NX + x) * NY + y


def steps_of(stage, core, r):
    if stage == "z":
        return (r, 0, 0)
    along_x = (stage == "first") == (core == 0)
    return (0, r, 0) if along_x else (0, 0, r)


def moved(a, stage, r):
    pairs = []
    for z in range(NZ):
        for x in range(NX):
            for y in range(NY):
                for j in range(N_BUS):
                    dz, dx, dy = steps_of(stage, j % 2, r)
                    to = band_index((z + dz) % NZ, (x + dx) % NX, (y + dy) % NY)
                    pairs.append((band_index(z, x, y) * N_BUS + j, to * N_BUS + j))
    return lax.ppermute(a, ("band", "bus"), pairs)


def gather_z(block):
    return jnp.concatenate([block, moved(block, "z", 1)], axis=0)


def gather_second(eight):
    one, three, two = (moved(eight, "second", -r) for r in (1, 3, 2))
    return [eight, one, two, three]


def ring_first(pair):
    one, three, two = (moved(pair, "first", -r) for r in (1, 3, 2))
    return pair, one, two, three


def gather_first(pair):
    return jnp.concatenate(ring_first(pair), axis=0)


def gather_second(eight):
    one, three, two = (moved(eight, "second", -r) for r in (1, 3, 2))
    return [eight, one, two, three]


def sum_bus(a):
    got = [
        lax.ppermute(a, "bus", [(j, j ^ k) for j in range(N_BUS)]) for k in (2, 3, 1)
    ]
    return (a + got[2]) + (got[0] + got[1])


def sum_band(chunks):
    got = [moved(chunks[r], "second", r) for r in (2, 1, 3)]
    eight = chunks[0] + got[0] + got[1] + got[2]
    n = eight.shape[0] // 4
    parts = [eight[r * n : (r + 1) * n] for r in range(4)]
    got = [moved(parts[r], "first", r) for r in (2, 1, 3)]
    return parts[0] + got[0] + got[1] + got[2]


def sum_z(pair, both):
    n = pair.shape[0] // 2
    if both:
        got = moved(pair, "z", 1)
        return pair + jnp.concatenate([got[n:], got[:n]], axis=0)
    return pair[:n] + moved(pair[n:], "z", 1)


def split(v):
    hi = v.astype(jnp.bfloat16)
    lo = (v - hi.astype(jnp.float32)).astype(jnp.bfloat16)
    return hi, lo


def three_pass(x, w, dims):
    x_hi, x_lo = split(x)
    w_hi, w_lo = split(w)
    n = x.shape[0]
    y = lax.dot_general(
        jnp.concatenate([x_hi, x_lo], axis=0), w_hi, dims, preferred_element_type=jnp.float32
    )
    return y[:n] + (
        y[n:] + lax.dot_general(x_hi, w_lo, dims, preferred_element_type=jnp.float32)
    )


def lanes(ref, count):
    n = ref.shape[0] // count
    return jnp.concatenate([ref[k * n : (k + 1) * n, :] for k in range(count)], axis=1)


def cost(us):
    return pl.CostEstimate(flops=0, bytes_accessed=int(us * 3.0e6), transcendentals=0)


BLOCK_ROWS = LOAD_ROWS + SLOT_ROWS
FIRST_STEP = 4


def first_flow_kernel(steps, idx_ref, at_ref, load_acc_ref, slot_acc_ref, columns_ref, *refs):
    *refs, load_ref, slot_ref = refs
    w_refs, x_refs = refs[:FIRST_STEP], refs[FIRST_STEP:]
    i = pl.program_id(0)

    @pl.when(i == 0)
    def _():
        load_ref[...] = load_acc_ref[...]
        slot_ref[...] = slot_acc_ref[...]

    def add(x_ref):
        load, slots = [], []
        for u in range(FIRST_STEP):
            base = u * BLOCK_ROWS
            load += [x_ref[base + k * S : base + (k + 1) * S, :] for k in range(SUB // 128)]
            base += LOAD_ROWS
            slots += [x_ref[base + k * S : base + (k + 1) * S, :] for k in range(CAP)]
        w = jnp.concatenate([ref[...] for ref in w_refs], axis=1)
        columns = columns_ref[...].reshape(FIRST_STEP * SLOTS, LINES_DEV)
        load_ref[...] -= three_pass(jnp.concatenate(load, axis=1), w, NT)
        slot_ref[...] += three_pass(jnp.concatenate(slots, axis=1), columns, NN)

    for k, x_ref in enumerate(x_refs):
        pl.when(i // steps == k)(lambda x_ref=x_ref: add(x_ref))


def first_flow(load_acc, slot_acc, xs, columns, ptdf, block_of, starts):
    steps = xs[0].shape[0] // (FIRST_STEP * BLOCK_ROWS)
    places = [start // FIRST_STEP + i for start in starts for i in range(steps)]
    order = jnp.concatenate(
        [block_of[start : start + steps * FIRST_STEP] for start in starts]
    )

    def sub(u):
        return pl.BlockSpec((LINES_DEV, SUB), lambda i, idx, at: (0, idx[i * FIRST_STEP + u]))

    def piece(k):
        return pl.BlockSpec(
            (FIRST_STEP * BLOCK_ROWS, 128),
            lambda i, idx, at: (jnp.clip(i - k * steps, 0, steps - 1), 0),
        )

    whole = pl.BlockSpec((S, LINES_DEV), lambda i, idx, at: (0, 0))
    return pl.pallas_call(
        functools.partial(first_flow_kernel, steps),
        grid_spec=pltpu.PrefetchScalarGridSpec(
            num_scalar_prefetch=2,
            grid=(len(places),),
            in_specs=[
                whole,
                whole,
                pl.BlockSpec((FIRST_STEP, SLOTS, LINES_DEV), lambda i, idx, at: (at[i], 0, 0)),
            ]
            + [sub(u) for u in range(FIRST_STEP)]
            + [piece(k) for k in range(len(xs))],
            out_specs=[whole] * 2,
        ),
        out_shape=[jax.ShapeDtypeStruct((S, LINES_DEV), jnp.float32)] * 2,
        compiler_params=pltpu.CompilerParams(vmem_limit_bytes=VMEM),
        cost_estimate=cost(3.0 * len(places)),
        name="first_flow",
    )(
        order,
        jnp.array(places, jnp.int32),
        load_acc,
        slot_acc,
        columns,
        *([ptdf] * FIRST_STEP),
        *xs,
    )


SLOT_STEPS = 2
SLOT_STEP = 8 // SLOT_STEPS


def slot_flow_kernel(acc_ref, x_ref, w_ref, o_ref):
    @pl.when(pl.program_id(0) == 0)
    def _():
        o_ref[...] = acc_ref[...]

    w = w_ref[...].reshape(SLOT_STEP * SLOTS, LINES_DEV)
    o_ref[...] += three_pass(lanes(x_ref, SLOT_STEP * CAP), w, NN)


def slot_flow(acc, x, columns, r2):
    s = acc.shape[0]
    return pl.pallas_call(
        slot_flow_kernel,
        grid=(SLOT_STEPS,),
        in_specs=[
            pl.BlockSpec((s, LINES_DEV), lambda i: (0, 0)),
            pl.BlockSpec((SLOT_STEP * CAP * s, 128), lambda i: (i, 0)),
            pl.BlockSpec(
                (SLOT_STEP, SLOTS, LINES_DEV), lambda i: (r2 * SLOT_STEPS + i, 0, 0)
            ),
        ],
        out_specs=pl.BlockSpec((s, LINES_DEV), lambda i: (0, 0)),
        out_shape=jax.ShapeDtypeStruct((s, LINES_DEV), jnp.float32),
        compiler_params=pltpu.CompilerParams(vmem_limit_bytes=VMEM),
        cost_estimate=cost(2.0),
        name="slot_flow",
    )(acc, x, columns)


def slot_price_kernel(x_ref, w_ref, *o_refs):
    w = w_ref[...].reshape(8 * SLOTS, LINES_DEV)
    p = three_pass(x_ref[...], w, NT)
    for step, o_ref in enumerate(o_refs):

        @pl.when(pl.program_id(0) == step)
        def _():
            for k in range(8 * CAP):
                o_ref[k * S : (k + 1) * S, :] = p[:, k * 128 : (k + 1) * 128]


def slot_price(x, columns, chunks):
    n, top = len(chunks), chunks[0]
    return pl.pallas_call(
        slot_price_kernel,
        grid=(n,),
        in_specs=[
            pl.BlockSpec((S, LINES_DEV), lambda i: (0, 0)),
            pl.BlockSpec((8, SLOTS, LINES_DEV), lambda i: (top - i, 0, 0)),
        ],
        out_specs=[pl.BlockSpec((8 * SLOT_ROWS, 128), lambda i: (0, 0))] * n,
        out_shape=[jax.ShapeDtypeStruct((8 * SLOT_ROWS, 128), jnp.float32)] * n,
        compiler_params=pltpu.CompilerParams(vmem_limit_bytes=VMEM),
        cost_estimate=cost(2.0 * n),
        name="slot_price",
    )(x, columns)


PICK_STEP = 4
HOT = CAP * N_BUS


def pick_kernel(code_ref, w_ref, o_ref):
    codes = code_ref[...]
    column = lax.broadcasted_iota(jnp.int32, codes.shape, 1)
    bus = lax.broadcasted_iota(jnp.int32, (SLOTS, SUB), 1).astype(jnp.float32) + 1.0
    for u in range(PICK_STEP):
        i = pl.program_id(0) * PICK_STEP + u
        w_hi, w_lo = split(w_ref[:, u * SUB : (u + 1) * SUB])
        code = jnp.sum(jnp.where(column == i, codes, 0.0), axis=1, keepdims=True)
        hot = (bus == code).astype(jnp.float32).astype(jnp.bfloat16)
        picked = lax.dot_general(hot, w_hi, NT, preferred_element_type=jnp.float32)
        picked += lax.dot_general(hot, w_lo, NT, preferred_element_type=jnp.float32)
        for b in range(N_BAND):
            for q in range(HOT):
                o_ref[b, pl.ds(q * N_BAND + i, 1), :] = picked[b * HOT + q : b * HOT + q + 1, :]


def pick(codes, ptdf):
    return pl.pallas_call(
        pick_kernel,
        grid=(N_BAND // PICK_STEP,),
        in_specs=[
            pl.BlockSpec((SLOTS, N_BAND), lambda i: (0, 0)),
            pl.BlockSpec((LINES_DEV, PICK_STEP * SUB), lambda i: (0, i)),
        ],
        out_specs=pl.BlockSpec((N_BAND, SLOTS, LINES_DEV), lambda i: (0, 0, 0)),
        out_shape=jax.ShapeDtypeStruct((N_BAND, SLOTS, LINES_DEV), jnp.float32),
        compiler_params=pltpu.CompilerParams(vmem_limit_bytes=VMEM),
        cost_estimate=cost(30.0),
        name="pick",
    )(codes, ptdf)


def home_columns(bus_map):
    owner = bus_map // SUB
    same = owner[:, None] == owner[None, :]
    earlier = lax.broadcasted_iota(jnp.int32, same.shape, 0) > lax.broadcasted_iota(
        jnp.int32, same.shape, 1
    )
    rank = jnp.sum((same & earlier).astype(jnp.int32), axis=1)
    return owner // N_BAND * 128 + rank * N_BAND + owner % N_BAND, bus_map % SUB


def exact_dot(a, b, dims):
    return lax.dot_general(
        a, b, dims, precision=lax.Precision.HIGHEST, preferred_element_type=jnp.float32
    )


def on_device(
    dispatch0, cost_lin, cost_quad, gen_max, bus_map, demand, ptdf, line_price0, flow_max
):
    band = lax.axis_index("band")
    core = lax.axis_index("bus") % 2
    z, x, y = band // (NX * NY), band // NY % NX, band % NY
    rel = lax.iota(jnp.int32, N_BAND)
    r2, r1, rz = rel // 8, rel // 2 % 4, rel % 2
    dx, dy = jnp.where(core == 0, r1, r2), jnp.where(core == 0, r2, r1)
    block_of = band_index((z + rz) % NZ, (x + dx) % NX, (y + dy) % NY)

    at, local = home_columns(bus_map)
    where = (at[:, None] == lax.broadcasted_iota(jnp.int32, (1, N_BUS * 128), 1)).astype(
        jnp.float32
    )
    own = jnp.concatenate(
        [
            dispatch0,
            (local + 1).astype(jnp.float32)[None],
            cost_lin[None],
            cost_quad[None],
            gen_max[None],
            jnp.zeros((4, dispatch0.shape[1]), jnp.float32),
        ],
        axis=0,
    )
    rows = own.shape[0]
    message = exact_dot(own, where, NN).reshape(rows, N_BUS, 128).transpose(1, 0, 2)
    got = lax.all_to_all(message, "bus", split_axis=0, concat_axis=0, tiled=True)
    got = got[:, :, : CAP * N_BAND].reshape(N_BUS, rows, CAP, N_BAND)
    got = got.transpose(2, 1, 0, 3).reshape(CAP, rows, 128)
    load = demand[:, 0, :].reshape(S, SUB // 128, 128).transpose(1, 0, 2)
    params = got[:, S + 1 : S + 4].transpose(1, 0, 2).reshape(3 * CAP, 128)
    both = gather_z(
        jnp.concatenate(
            [
                load.reshape(LOAD_ROWS, 128),
                got[:, :S].reshape(SLOT_ROWS, 128),
                jnp.pad(params, ((0, 16 - 3 * CAP), (0, 0))),
            ],
            axis=0,
        )
    )
    codes = jnp.pad(got[:, S], ((0, 8 - CAP), (0, 0)))
    codes = lax.all_to_all(
        jnp.broadcast_to(codes, (N_BAND, 8, 128)), "band", split_axis=0, concat_axis=0, tiled=True
    )
    codes = codes[:, :CAP][block_of].reshape(SLOTS, N_BAND)
    both = both.reshape(2, BLOCK_ROWS + 16, 128)
    params = both[:, BLOCK_ROWS : BLOCK_ROWS + 3 * CAP].reshape(2, 3, CAP, 1, 128)
    lin, quad, top = (params[:, k] for k in range(3))
    now = both[:, LOAD_ROWS:BLOCK_ROWS].reshape(2, CAP, S, 128)
    eight = gather_first(both[:, :BLOCK_ROWS].reshape(2 * BLOCK_ROWS, 128))
    eight, codes = lax.optimization_barrier((eight, codes))
    columns = pick(codes, ptdf)
    one, three = moved(eight, "second", -1), moved(eight, "second", -3)
    one, three, columns = lax.optimization_barrier((one, three, columns))
    n = eight.shape[0] // 2
    two_near, two_far = moved(one[:n], "second", -1), moved(three[n:], "second", -3)
    load_part = slot_part = jnp.zeros((S, LINES_DEV), jnp.float32)
    for xs, starts in (((eight, one, three), (0, 8, 24)), ((two_near, two_far), (16, 20))):
        load_part, slot_part = first_flow(
            load_part, slot_part, xs, columns, ptdf, block_of, starts
        )
    flow = load_part + slot_part

    bound = dual_step * flow_max
    line_price = line_price0
    for iteration in range(ITERS):
        last = iteration == ITERS - 1
        trial = line_price + dual_step * sum_bus(flow)
        price_next = trial - jnp.clip(trial, -bound, bound)
        reflected = 2.0 * price_next - line_price
        line_price = price_next
        three, two, one = slot_price(reflected, columns, (3, 2, 1))
        chunks = [*slot_price(reflected, columns, (0,)), one, two, three]
        unit = sum_z(sum_band(chunks), not last)
        unit = unit.reshape(-1, CAP, S, 128)
        k = unit.shape[0]
        before = now[:k]
        now = jnp.clip(
            (before - primal_step * (lin[:k] + unit)) / (1.0 + primal_step * quad[:k]),
            0.0,
            top[:k],
        )
        if not last:
            slots = gather_second(gather_first(now.reshape(2 * SLOT_ROWS, 128)))
            flow = load_part
            for r in (0, 1, 3, 2):
                flow = slot_flow(flow, slots[r], columns, r)
    slot_values = now[0]
    home = slot_values.reshape(CAP, S, N_BUS, N_BAND).transpose(2, 1, 0, 3)
    home = home.reshape(N_BUS, S, CAP * N_BAND)
    home = jnp.pad(home, ((0, 0), (0, 0), (0, 128 - CAP * N_BAND)))
    home = lax.all_to_all(home, "bus", split_axis=0, concat_axis=0, tiled=True)
    dispatch = exact_dot(home.transpose(1, 0, 2).reshape(S, N_BUS * 128), where, NT)
    return dispatch, line_price


def solution(mesh):
    gens = P(("band", "bus"))
    in_specs = (
        P(None, ("band", "bus")),
        gens,
        gens,
        gens,
        gens,
        P(None, "bus", "band"),
        P("band", "bus"),
        P(None, "band"),
        P("band"),
    )
    out_specs = (P(None, ("band", "bus")), P(None, "band"))
    return jax.shard_map(
        on_device, mesh=mesh, in_specs=in_specs, out_specs=out_specs, check_vma=False
    )
```

```python
import functools

import jax
import jax.numpy as jnp
from jax import lax
from jax.experimental import pallas as pl
from jax.experimental.pallas import tpu as pltpu
from jax.sharding import PartitionSpec as P

ITERS = 2
S = 64
SUB = 768
CAP = 3
N_BUS = 4
N_BAND = 32
SLOTS = CAP * 128
LINES_DEV = 256
LOAD_ROWS = SUB // 128 * S
SLOT_ROWS = CAP * S

primal_step = 0.5
dual_step = 1.0

NZ, NX, NY = 2, 4, 4
NT = (((1,), (1,)), ((), ()))
NN = (((1,), (0,)), ((), ()))
VMEM = 48 * 1024 * 1024


def band_index(z, x, y):
    return (z * NX + x) * NY + y


def steps_of(stage, core, r):
    if stage == "z":
        return (r, 0, 0)
    along_x = (stage == "first") == (core == 0)
    return (0, r, 0) if along_x else (0, 0, r)


def moved(a, stage, r):
    pairs = []
    for z in range(NZ):
        for x in range(NX):
            for y in range(NY):
                for j in range(N_BUS):
                    dz, dx, dy = steps_of(stage, j % 2, r)
                    to = band_index((z + dz) % NZ, (x + dx) % NX, (y + dy) % NY)
                    pairs.append((band_index(z, x, y) * N_BUS + j, to * N_BUS + j))
    return lax.ppermute(a, ("band", "bus"), pairs)


def gather_z(block):
    return jnp.concatenate([block, moved(block, "z", 1)], axis=0)


def gather_second(eight):
    one, three, two = (moved(eight, "second", -r) for r in (1, 3, 2))
    return [eight, one, two, three]


def ring_first(pair):
    one, three, two = (moved(pair, "first", -r) for r in (1, 3, 2))
    return pair, one, two, three


def gather_first(pair):
    return jnp.concatenate(ring_first(pair), axis=0)


def gather_second(eight):
    one, three, two = (moved(eight, "second", -r) for r in (1, 3, 2))
    return [eight, one, two, three]


def sum_bus(a):
    got = [
        lax.ppermute(a, "bus", [(j, j ^ k) for j in range(N_BUS)]) for k in (2, 3, 1)
    ]
    return (a + got[2]) + (got[0] + got[1])


def sum_band(chunks):
    got = [moved(chunks[r], "second", r) for r in (2, 1, 3)]
    eight = chunks[0] + got[0] + got[1] + got[2]
    n = eight.shape[0] // 4
    parts = [eight[r * n : (r + 1) * n] for r in range(4)]
    got = [moved(parts[r], "first", r) for r in (2, 1, 3)]
    return parts[0] + got[0] + got[1] + got[2]


def sum_z(pair, both):
    n = pair.shape[0] // 2
    if both:
        got = moved(pair, "z", 1)
        return pair + jnp.concatenate([got[n:], got[:n]], axis=0)
    return pair[:n] + moved(pair[n:], "z", 1)


def split(v):
    hi = v.astype(jnp.bfloat16)
    lo = (v - hi.astype(jnp.float32)).astype(jnp.bfloat16)
    return hi, lo


def three_pass(x, w, dims):
    x_hi, x_lo = split(x)
    w_hi, w_lo = split(w)
    n = x.shape[0]
    y = lax.dot_general(
        jnp.concatenate([x_hi, x_lo], axis=0), w_hi, dims, preferred_element_type=jnp.float32
    )
    return y[:n] + (
        y[n:] + lax.dot_general(x_hi, w_lo, dims, preferred_element_type=jnp.float32)
    )


def lanes(ref, count):
    n = ref.shape[0] // count
    return jnp.concatenate([ref[k * n : (k + 1) * n, :] for k in range(count)], axis=1)


def cost(us):
    return pl.CostEstimate(flops=0, bytes_accessed=int(us * 3.0e6), transcendentals=0)


BLOCK_ROWS = LOAD_ROWS + SLOT_ROWS
FIRST_STEP = 4


def first_flow_kernel(steps, idx_ref, at_ref, load_acc_ref, slot_acc_ref, columns_ref, *refs):
    *refs, load_ref, slot_ref = refs
    w_refs, x_refs = refs[:FIRST_STEP], refs[FIRST_STEP:]
    i = pl.program_id(0)

    @pl.when(i == 0)
    def _():
        load_ref[...] = load_acc_ref[...]
        slot_ref[...] = slot_acc_ref[...]

    def add(x_ref):
        load, slots = [], []
        for u in range(FIRST_STEP):
            base = u * BLOCK_ROWS
            load += [x_ref[base + k * S : base + (k + 1) * S, :] for k in range(SUB // 128)]
            base += LOAD_ROWS
            slots += [x_ref[base + k * S : base + (k + 1) * S, :] for k in range(CAP)]
        w = jnp.concatenate([ref[...] for ref in w_refs], axis=1)
        columns = columns_ref[...].reshape(FIRST_STEP * SLOTS, LINES_DEV)
        load_ref[...] -= three_pass(jnp.concatenate(load, axis=1), w, NT)
        slot_ref[...] += three_pass(jnp.concatenate(slots, axis=1), columns, NN)

    for k, x_ref in enumerate(x_refs):
        pl.when(i // steps == k)(lambda x_ref=x_ref: add(x_ref))


def first_flow(load_acc, slot_acc, xs, columns, ptdf, block_of, starts):
    steps = xs[0].shape[0] // (FIRST_STEP * BLOCK_ROWS)
    places = [start // FIRST_STEP + i for start in starts for i in range(steps)]
    order = jnp.concatenate(
        [block_of[start : start + steps * FIRST_STEP] for start in starts]
    )

    def sub(u):
        return pl.BlockSpec((LINES_DEV, SUB), lambda i, idx, at: (0, idx[i * FIRST_STEP + u]))

    def piece(k):
        return pl.BlockSpec(
            (FIRST_STEP * BLOCK_ROWS, 128),
            lambda i, idx, at: (jnp.clip(i - k * steps, 0, steps - 1), 0),
        )

    whole = pl.BlockSpec((S, LINES_DEV), lambda i, idx, at: (0, 0))
    return pl.pallas_call(
        functools.partial(first_flow_kernel, steps),
        grid_spec=pltpu.PrefetchScalarGridSpec(
            num_scalar_prefetch=2,
            grid=(len(places),),
            in_specs=[
                whole,
                whole,
                pl.BlockSpec((FIRST_STEP, SLOTS, LINES_DEV), lambda i, idx, at: (at[i], 0, 0)),
            ]
            + [sub(u) for u in range(FIRST_STEP)]
            + [piece(k) for k in range(len(xs))],
            out_specs=[whole] * 2,
        ),
        out_shape=[jax.ShapeDtypeStruct((S, LINES_DEV), jnp.float32)] * 2,
        compiler_params=pltpu.CompilerParams(vmem_limit_bytes=VMEM),
        cost_estimate=cost(3.0 * len(places)),
        name="first_flow",
    )(
        order,
        jnp.array(places, jnp.int32),
        load_acc,
        slot_acc,
        columns,
        *([ptdf] * FIRST_STEP),
        *xs,
    )


SLOT_STEPS = 2
SLOT_STEP = 8 // SLOT_STEPS


def slot_flow_kernel(acc_ref, x_ref, w_ref, o_ref):
    @pl.when(pl.program_id(0) == 0)
    def _():
        o_ref[...] = acc_ref[...]

    w = w_ref[...].reshape(SLOT_STEP * SLOTS, LINES_DEV)
    o_ref[...] += three_pass(lanes(x_ref, SLOT_STEP * CAP), w, NN)


def slot_flow(acc, x, columns, r2):
    s = acc.shape[0]
    return pl.pallas_call(
        slot_flow_kernel,
        grid=(SLOT_STEPS,),
        in_specs=[
            pl.BlockSpec((s, LINES_DEV), lambda i: (0, 0)),
            pl.BlockSpec((SLOT_STEP * CAP * s, 128), lambda i: (i, 0)),
            pl.BlockSpec(
                (SLOT_STEP, SLOTS, LINES_DEV), lambda i: (r2 * SLOT_STEPS + i, 0, 0)
            ),
        ],
        out_specs=pl.BlockSpec((s, LINES_DEV), lambda i: (0, 0)),
        out_shape=jax.ShapeDtypeStruct((s, LINES_DEV), jnp.float32),
        compiler_params=pltpu.CompilerParams(vmem_limit_bytes=VMEM),
        cost_estimate=cost(2.0),
        name="slot_flow",
    )(acc, x, columns)


def slot_price_kernel(x_ref, w_ref, *o_refs):
    w = w_ref[...].reshape(8 * SLOTS, LINES_DEV)
    p = three_pass(x_ref[...], w, NT)
    for step, o_ref in enumerate(o_refs):

        @pl.when(pl.program_id(0) == step)
        def _():
            for k in range(8 * CAP):
                o_ref[k * S : (k + 1) * S, :] = p[:, k * 128 : (k + 1) * 128]


def slot_price(x, columns, chunks):
    n, top = len(chunks), chunks[0]
    return pl.pallas_call(
        slot_price_kernel,
        grid=(n,),
        in_specs=[
            pl.BlockSpec((S, LINES_DEV), lambda i: (0, 0)),
            pl.BlockSpec((8, SLOTS, LINES_DEV), lambda i: (top - i, 0, 0)),
        ],
        out_specs=[pl.BlockSpec((8 * SLOT_ROWS, 128), lambda i: (0, 0))] * n,
        out_shape=[jax.ShapeDtypeStruct((8 * SLOT_ROWS, 128), jnp.float32)] * n,
        compiler_params=pltpu.CompilerParams(vmem_limit_bytes=VMEM),
        cost_estimate=cost(2.0 * n),
        name="slot_price",
    )(x, columns)


PICK_STEP = 4
HOT = CAP * N_BUS


def pick_kernel(code_ref, w_ref, o_ref):
    codes = code_ref[...]
    column = lax.broadcasted_iota(jnp.int32, codes.shape, 1)
    bus = lax.broadcasted_iota(jnp.int32, (SLOTS, SUB), 1).astype(jnp.float32) + 1.0
    for u in range(PICK_STEP):
        i = pl.program_id(0) * PICK_STEP + u
        w_hi, w_lo = split(w_ref[:, u * SUB : (u + 1) * SUB])
        code = jnp.sum(jnp.where(column == i, codes, 0.0), axis=1, keepdims=True)
        hot = (bus == code).astype(jnp.float32).astype(jnp.bfloat16)
        picked = lax.dot_general(hot, w_hi, NT, preferred_element_type=jnp.float32)
        picked += lax.dot_general(hot, w_lo, NT, preferred_element_type=jnp.float32)
        for b in range(N_BAND):
            for q in range(HOT):
                o_ref[b, pl.ds(q * N_BAND + i, 1), :] = picked[b * HOT + q : b * HOT + q + 1, :]


def pick(codes, ptdf):
    return pl.pallas_call(
        pick_kernel,
        grid=(N_BAND // PICK_STEP,),
        in_specs=[
            pl.BlockSpec((SLOTS, N_BAND), lambda i: (0, 0)),
            pl.BlockSpec((LINES_DEV, PICK_STEP * SUB), lambda i: (0, i)),
        ],
        out_specs=pl.BlockSpec((N_BAND, SLOTS, LINES_DEV), lambda i: (0, 0, 0)),
        out_shape=jax.ShapeDtypeStruct((N_BAND, SLOTS, LINES_DEV), jnp.float32),
        compiler_params=pltpu.CompilerParams(vmem_limit_bytes=VMEM),
        cost_estimate=cost(30.0),
        name="pick",
    )(codes, ptdf)


def exchange_bus(parts):
    return [parts[0]] + [
        lax.ppermute(parts[k], "bus", [(j, j ^ k) for j in range(N_BUS)]) for k in (1, 2, 3)
    ]


def home_columns(bus_map, place):
    owner = bus_map // SUB
    same = owner[:, None] == owner[None, :]
    earlier = lax.broadcasted_iota(jnp.int32, same.shape, 0) > lax.broadcasted_iota(
        jnp.int32, same.shape, 1
    )
    rank = jnp.sum((same & earlier).astype(jnp.int32), axis=1)
    return (owner // N_BAND ^ place) * 128 + rank * N_BAND + owner % N_BAND, bus_map % SUB


def exact_dot(a, b, dims):
    return lax.dot_general(
        a, b, dims, precision=lax.Precision.HIGHEST, preferred_element_type=jnp.float32
    )


def on_device(
    dispatch0, cost_lin, cost_quad, gen_max, bus_map, demand, ptdf, line_price0, flow_max
):
    band = lax.axis_index("band")
    place = lax.axis_index("bus")
    core = place % 2
    z, x, y = band // (NX * NY), band // NY % NX, band % NY
    rel = lax.iota(jnp.int32, N_BAND)
    r2, r1, rz = rel // 8, rel // 2 % 4, rel % 2
    dx, dy = jnp.where(core == 0, r1, r2), jnp.where(core == 0, r2, r1)
    block_of = band_index((z + rz) % NZ, (x + dx) % NX, (y + dy) % NY)

    at, local = home_columns(bus_map, place)
    where = (at[:, None] == lax.broadcasted_iota(jnp.int32, (1, N_BUS * 128), 1)).astype(
        jnp.float32
    )
    own = jnp.concatenate(
        [
            dispatch0,
            (local + 1).astype(jnp.float32)[None],
            cost_lin[None],
            cost_quad[None],
            gen_max[None],
            jnp.zeros((4, dispatch0.shape[1]), jnp.float32),
        ],
        axis=0,
    )
    rows = own.shape[0]
    message = exact_dot(own, where, NN)
    got = jnp.stack(exchange_bus([message[:, k * 128 : (k + 1) * 128] for k in range(N_BUS)]))
    got = got[:, :, : CAP * N_BAND].reshape(N_BUS, rows, CAP, N_BAND)
    got = got.transpose(2, 1, 0, 3).reshape(CAP, rows, 128)
    load = demand[:, 0, :].reshape(S, SUB // 128, 128).transpose(1, 0, 2)
    params = got[:, S + 1 : S + 4].transpose(1, 0, 2).reshape(3 * CAP, 128)
    both = gather_z(
        jnp.concatenate(
            [
                load.reshape(LOAD_ROWS, 128),
                got[:, :S].reshape(SLOT_ROWS, 128),
                jnp.pad(params, ((0, 16 - 3 * CAP), (0, 0))),
            ],
            axis=0,
        )
    )
    codes = jnp.pad(got[:, S], ((0, 8 - CAP), (0, 0)))
    codes = lax.all_to_all(
        jnp.broadcast_to(codes, (N_BAND, 8, 128)), "band", split_axis=0, concat_axis=0, tiled=True
    )
    codes = codes[:, :CAP][block_of].reshape(SLOTS, N_BAND)
    both, codes = lax.optimization_barrier((both, codes))
    both = both.reshape(2, BLOCK_ROWS + 16, 128)
    params = both[:, BLOCK_ROWS : BLOCK_ROWS + 3 * CAP].reshape(2, 3, CAP, 1, 128)
    lin, quad, top = (params[:, k] for k in range(3))
    now = both[:, LOAD_ROWS:BLOCK_ROWS].reshape(2, CAP, S, 128)
    eight = gather_first(both[:, :BLOCK_ROWS].reshape(2 * BLOCK_ROWS, 128))
    eight, codes = lax.optimization_barrier((eight, codes))
    columns = pick(codes, ptdf)
    one, three = moved(eight, "second", -1), moved(eight, "second", -3)
    one, three, columns = lax.optimization_barrier((one, three, columns))
    n = eight.shape[0] // 2
    two_near, two_far = moved(one[:n], "second", -1), moved(three[n:], "second", -3)
    load_part = slot_part = jnp.zeros((S, LINES_DEV), jnp.float32)
    for xs, starts in (((eight, one, three), (0, 8, 24)), ((two_near, two_far), (16, 20))):
        load_part, slot_part = first_flow(
            load_part, slot_part, xs, columns, ptdf, block_of, starts
        )
    flow = load_part + slot_part

    bound = dual_step * flow_max
    line_price = line_price0
    for iteration in range(ITERS):
        last = iteration == ITERS - 1
        trial = line_price + dual_step * sum_bus(flow)
        price_next = trial - jnp.clip(trial, -bound, bound)
        reflected = 2.0 * price_next - line_price
        line_price = price_next
        three, two, one = slot_price(reflected, columns, (3, 2, 1))
        chunks = [*slot_price(reflected, columns, (0,)), one, two, three]
        unit = sum_z(sum_band(chunks), not last)
        unit = unit.reshape(-1, CAP, S, 128)
        k = unit.shape[0]
        before = now[:k]
        now = jnp.clip(
            (before - primal_step * (lin[:k] + unit)) / (1.0 + primal_step * quad[:k]),
            0.0,
            top[:k],
        )
        if not last:
            slots = gather_second(gather_first(now.reshape(2 * SLOT_ROWS, 128)))
            flow = load_part
            for r in (0, 1, 3, 2):
                flow = slot_flow(flow, slots[r], columns, r)
    slot_values = now[0]
    home = slot_values.reshape(CAP, S, N_BUS, N_BAND).transpose(2, 1, 0, 3)
    home = home.reshape(N_BUS, S, CAP * N_BAND)
    home = jnp.pad(home, ((0, 0), (0, 0), (0, 128 - CAP * N_BAND)))
    home = jnp.concatenate(exchange_bus([home[k] for k in range(N_BUS)]), axis=1)
    dispatch = exact_dot(home, where, NT)
    return dispatch, line_price


def solution(mesh):
    gens = P(("band", "bus"))
    in_specs = (
        P(None, ("band", "bus")),
        gens,
        gens,
        gens,
        gens,
        P(None, "bus", "band"),
        P("band", "bus"),
        P(None, "band"),
        P("band"),
    )
    out_specs = (P(None, ("band", "bus")), P(None, "band"))
    return jax.shard_map(
        on_device, mesh=mesh, in_specs=in_specs, out_specs=out_specs, check_vma=False
    )
```

```python
import functools

import jax
import jax.numpy as jnp
from jax import lax
from jax.experimental import pallas as pl
from jax.experimental.pallas import tpu as pltpu
from jax.sharding import PartitionSpec as P

ITERS = 2
S = 64
SUB = 768
CAP = 3
N_BUS = 4
N_BAND = 32
SLOTS = CAP * 128
LINES_DEV = 256
LOAD_ROWS = SUB // 128 * S
SLOT_ROWS = CAP * S

primal_step = 0.5
dual_step = 1.0

NZ, NX, NY = 2, 4, 4
NT = (((1,), (1,)), ((), ()))
NN = (((1,), (0,)), ((), ()))
VMEM = 48 * 1024 * 1024


def band_index(z, x, y):
    return (z * NX + x) * NY + y


def steps_of(stage, core, r):
    if stage == "z":
        return (r, 0, 0)
    along_x = (stage == "first") == (core == 0)
    return (0, r, 0) if along_x else (0, 0, r)


def moved(a, stage, r):
    pairs = []
    for z in range(NZ):
        for x in range(NX):
            for y in range(NY):
                for j in range(N_BUS):
                    dz, dx, dy = steps_of(stage, j % 2, r)
                    to = band_index((z + dz) % NZ, (x + dx) % NX, (y + dy) % NY)
                    pairs.append((band_index(z, x, y) * N_BUS + j, to * N_BUS + j))
    return lax.ppermute(a, ("band", "bus"), pairs)


def gather_z(block):
    return jnp.concatenate([block, moved(block, "z", 1)], axis=0)


def gather_second(eight):
    one, three, two = (moved(eight, "second", -r) for r in (1, 3, 2))
    return [eight, one, two, three]


def ring_first(pair):
    one, three, two = (moved(pair, "first", -r) for r in (1, 3, 2))
    return pair, one, two, three


def gather_first(pair):
    return jnp.concatenate(ring_first(pair), axis=0)


def gather_second(eight):
    one, three, two = (moved(eight, "second", -r) for r in (1, 3, 2))
    return [eight, one, two, three]


def sum_bus(a):
    got = [
        lax.ppermute(a, "bus", [(j, j ^ k) for j in range(N_BUS)]) for k in (2, 3, 1)
    ]
    return (a + got[2]) + (got[0] + got[1])


def sum_band(chunks):
    got = [moved(chunks[r], "second", r) for r in (2, 1, 3)]
    eight = chunks[0] + got[0] + got[1] + got[2]
    n = eight.shape[0] // 4
    parts = [eight[r * n : (r + 1) * n] for r in range(4)]
    got = [moved(parts[r], "first", r) for r in (2, 1, 3)]
    return parts[0] + got[0] + got[1] + got[2]


def sum_z(pair, both):
    n = pair.shape[0] // 2
    if both:
        got = moved(pair, "z", 1)
        return pair + jnp.concatenate([got[n:], got[:n]], axis=0)
    return pair[:n] + moved(pair[n:], "z", 1)


def split(v):
    hi = v.astype(jnp.bfloat16)
    lo = (v - hi.astype(jnp.float32)).astype(jnp.bfloat16)
    return hi, lo


def three_pass(x, w, dims):
    x_hi, x_lo = split(x)
    w_hi, w_lo = split(w)
    n = x.shape[0]
    y = lax.dot_general(
        jnp.concatenate([x_hi, x_lo], axis=0), w_hi, dims, preferred_element_type=jnp.float32
    )
    return y[:n] + (
        y[n:] + lax.dot_general(x_hi, w_lo, dims, preferred_element_type=jnp.float32)
    )


def lanes(ref, count):
    n = ref.shape[0] // count
    return jnp.concatenate([ref[k * n : (k + 1) * n, :] for k in range(count)], axis=1)


def cost(us):
    return pl.CostEstimate(flops=0, bytes_accessed=int(us * 3.0e6), transcendentals=0)


BLOCK_ROWS = LOAD_ROWS + SLOT_ROWS
FIRST_STEP = 4


def first_flow_kernel(steps, idx_ref, at_ref, load_acc_ref, slot_acc_ref, columns_ref, *refs):
    *refs, load_ref, slot_ref = refs
    w_refs, x_refs = refs[:FIRST_STEP], refs[FIRST_STEP:]
    i = pl.program_id(0)

    @pl.when(i == 0)
    def _():
        load_ref[...] = load_acc_ref[...]
        slot_ref[...] = slot_acc_ref[...]

    def add(x_ref):
        load, slots = [], []
        for u in range(FIRST_STEP):
            base = u * BLOCK_ROWS
            load += [x_ref[base + k * S : base + (k + 1) * S, :] for k in range(SUB // 128)]
            base += LOAD_ROWS
            slots += [x_ref[base + k * S : base + (k + 1) * S, :] for k in range(CAP)]
        w = jnp.concatenate([ref[...] for ref in w_refs], axis=1)
        columns = columns_ref[...].reshape(FIRST_STEP * SLOTS, LINES_DEV)
        load_ref[...] -= three_pass(jnp.concatenate(load, axis=1), w, NT)
        slot_ref[...] += three_pass(jnp.concatenate(slots, axis=1), columns, NN)

    for k, x_ref in enumerate(x_refs):
        pl.when(i // steps == k)(lambda x_ref=x_ref: add(x_ref))


def first_flow(load_acc, slot_acc, xs, columns, ptdf, block_of, starts):
    steps = xs[0].shape[0] // (FIRST_STEP * BLOCK_ROWS)
    places = [start // FIRST_STEP + i for start in starts for i in range(steps)]
    order = jnp.concatenate(
        [block_of[start : start + steps * FIRST_STEP] for start in starts]
    )

    def sub(u):
        return pl.BlockSpec((LINES_DEV, SUB), lambda i, idx, at: (0, idx[i * FIRST_STEP + u]))

    def piece(k):
        return pl.BlockSpec(
            (FIRST_STEP * BLOCK_ROWS, 128),
            lambda i, idx, at: (jnp.clip(i - k * steps, 0, steps - 1), 0),
        )

    whole = pl.BlockSpec((S, LINES_DEV), lambda i, idx, at: (0, 0))
    return pl.pallas_call(
        functools.partial(first_flow_kernel, steps),
        grid_spec=pltpu.PrefetchScalarGridSpec(
            num_scalar_prefetch=2,
            grid=(len(places),),
            in_specs=[
                whole,
                whole,
                pl.BlockSpec((FIRST_STEP, SLOTS, LINES_DEV), lambda i, idx, at: (at[i], 0, 0)),
            ]
            + [sub(u) for u in range(FIRST_STEP)]
            + [piece(k) for k in range(len(xs))],
            out_specs=[whole] * 2,
        ),
        out_shape=[jax.ShapeDtypeStruct((S, LINES_DEV), jnp.float32)] * 2,
        compiler_params=pltpu.CompilerParams(vmem_limit_bytes=VMEM),
        cost_estimate=cost(3.0 * len(places)),
        name="first_flow",
    )(
        order,
        jnp.array(places, jnp.int32),
        load_acc,
        slot_acc,
        columns,
        *([ptdf] * FIRST_STEP),
        *xs,
    )


SLOT_STEPS = 2
SLOT_STEP = 8 // SLOT_STEPS


def slot_flow_kernel(acc_ref, x_ref, w_ref, o_ref):
    @pl.when(pl.program_id(0) == 0)
    def _():
        o_ref[...] = acc_ref[...]

    w = w_ref[...].reshape(SLOT_STEP * SLOTS, LINES_DEV)
    o_ref[...] += three_pass(lanes(x_ref, SLOT_STEP * CAP), w, NN)


def slot_flow(acc, x, columns, r2):
    s = acc.shape[0]
    return pl.pallas_call(
        slot_flow_kernel,
        grid=(SLOT_STEPS,),
        in_specs=[
            pl.BlockSpec((s, LINES_DEV), lambda i: (0, 0)),
            pl.BlockSpec((SLOT_STEP * CAP * s, 128), lambda i: (i, 0)),
            pl.BlockSpec(
                (SLOT_STEP, SLOTS, LINES_DEV), lambda i: (r2 * SLOT_STEPS + i, 0, 0)
            ),
        ],
        out_specs=pl.BlockSpec((s, LINES_DEV), lambda i: (0, 0)),
        out_shape=jax.ShapeDtypeStruct((s, LINES_DEV), jnp.float32),
        compiler_params=pltpu.CompilerParams(vmem_limit_bytes=VMEM),
        cost_estimate=cost(2.0),
        name="slot_flow",
    )(acc, x, columns)


def slot_price_kernel(x_ref, w_ref, *o_refs):
    w = w_ref[...].reshape(8 * SLOTS, LINES_DEV)
    p = three_pass(x_ref[...], w, NT)
    for step, o_ref in enumerate(o_refs):

        @pl.when(pl.program_id(0) == step)
        def _():
            for k in range(8 * CAP):
                o_ref[k * S : (k + 1) * S, :] = p[:, k * 128 : (k + 1) * 128]


def slot_price(x, columns, chunks):
    n, top = len(chunks), chunks[0]
    return pl.pallas_call(
        slot_price_kernel,
        grid=(n,),
        in_specs=[
            pl.BlockSpec((S, LINES_DEV), lambda i: (0, 0)),
            pl.BlockSpec((8, SLOTS, LINES_DEV), lambda i: (top - i, 0, 0)),
        ],
        out_specs=[pl.BlockSpec((8 * SLOT_ROWS, 128), lambda i: (0, 0))] * n,
        out_shape=[jax.ShapeDtypeStruct((8 * SLOT_ROWS, 128), jnp.float32)] * n,
        compiler_params=pltpu.CompilerParams(vmem_limit_bytes=VMEM),
        cost_estimate=cost(2.0 * n),
        name="slot_price",
    )(x, columns)


PICK_STEP = 4
HOT = CAP * N_BUS


def pick_kernel(code_ref, w_ref, o_ref):
    codes = code_ref[...]
    column = lax.broadcasted_iota(jnp.int32, codes.shape, 1)
    bus = lax.broadcasted_iota(jnp.int32, (SLOTS, SUB), 1).astype(jnp.float32) + 1.0
    for u in range(PICK_STEP):
        i = pl.program_id(0) * PICK_STEP + u
        w_hi, w_lo = split(w_ref[:, u * SUB : (u + 1) * SUB])
        code = jnp.sum(jnp.where(column == i, codes, 0.0), axis=1, keepdims=True)
        hot = (bus == code).astype(jnp.float32).astype(jnp.bfloat16)
        picked = lax.dot_general(hot, w_hi, NT, preferred_element_type=jnp.float32)
        picked += lax.dot_general(hot, w_lo, NT, preferred_element_type=jnp.float32)
        for b in range(N_BAND):
            for q in range(HOT):
                o_ref[b, pl.ds(q * N_BAND + i, 1), :] = picked[b * HOT + q : b * HOT + q + 1, :]


def pick(codes, ptdf):
    return pl.pallas_call(
        pick_kernel,
        grid=(N_BAND // PICK_STEP,),
        in_specs=[
            pl.BlockSpec((SLOTS, N_BAND), lambda i: (0, 0)),
            pl.BlockSpec((LINES_DEV, PICK_STEP * SUB), lambda i: (0, i)),
        ],
        out_specs=pl.BlockSpec((N_BAND, SLOTS, LINES_DEV), lambda i: (0, 0, 0)),
        out_shape=jax.ShapeDtypeStruct((N_BAND, SLOTS, LINES_DEV), jnp.float32),
        compiler_params=pltpu.CompilerParams(vmem_limit_bytes=VMEM),
        cost_estimate=cost(30.0),
        name="pick",
    )(codes, ptdf)


def exchange_bus(parts):
    return [parts[0]] + [
        lax.ppermute(parts[k], "bus", [(j, j ^ k) for j in range(N_BUS)]) for k in (1, 2, 3)
    ]


def home_columns(bus_map, place):
    owner = bus_map // SUB
    same = owner[:, None] == owner[None, :]
    earlier = lax.broadcasted_iota(jnp.int32, same.shape, 0) > lax.broadcasted_iota(
        jnp.int32, same.shape, 1
    )
    rank = jnp.sum((same & earlier).astype(jnp.int32), axis=1)
    return (owner // N_BAND ^ place) * 128 + rank * N_BAND + owner % N_BAND, bus_map % SUB


def exact_dot(a, b, dims):
    return lax.dot_general(
        a, b, dims, precision=lax.Precision.HIGHEST, preferred_element_type=jnp.float32
    )


def on_device(
    dispatch0, cost_lin, cost_quad, gen_max, bus_map, demand, ptdf, line_price0, flow_max
):
    band = lax.axis_index("band")
    place = lax.axis_index("bus")
    core = place % 2
    z, x, y = band // (NX * NY), band // NY % NX, band % NY
    rel = lax.iota(jnp.int32, N_BAND)
    r2, r1, rz = rel // 8, rel // 2 % 4, rel % 2
    dx, dy = jnp.where(core == 0, r1, r2), jnp.where(core == 0, r2, r1)
    block_of = band_index((z + rz) % NZ, (x + dx) % NX, (y + dy) % NY)

    at, local = home_columns(bus_map, place)
    where = (at[:, None] == lax.broadcasted_iota(jnp.int32, (1, N_BUS * 128), 1)).astype(
        jnp.float32
    )
    own = jnp.concatenate(
        [
            dispatch0,
            (local + 1).astype(jnp.float32)[None],
            cost_lin[None],
            cost_quad[None],
            gen_max[None],
            jnp.zeros((4, dispatch0.shape[1]), jnp.float32),
        ],
        axis=0,
    )
    rows = own.shape[0]
    message = exact_dot(own, where, NN)
    got = jnp.stack(exchange_bus([message[:, k * 128 : (k + 1) * 128] for k in range(N_BUS)]))
    got = got[:, :, : CAP * N_BAND].reshape(N_BUS, rows, CAP, N_BAND)
    got = got.transpose(2, 1, 0, 3).reshape(CAP, rows, 128)
    load = demand[:, 0, :].reshape(S, SUB // 128, 128).transpose(1, 0, 2)
    params = got[:, S + 1 : S + 4].transpose(1, 0, 2).reshape(3 * CAP, 128)
    both = gather_z(
        jnp.concatenate(
            [
                load.reshape(LOAD_ROWS, 128),
                got[:, :S].reshape(SLOT_ROWS, 128),
                jnp.pad(params, ((0, 16 - 3 * CAP), (0, 0))),
            ],
            axis=0,
        )
    )
    codes = jnp.pad(got[:, S], ((0, 8 - CAP), (0, 0)))
    codes = lax.all_to_all(
        jnp.broadcast_to(codes, (N_BAND, 8, 128)), "band", split_axis=0, concat_axis=0, tiled=True
    )
    codes = codes[:, :CAP][block_of].reshape(SLOTS, N_BAND)
    both, codes = lax.optimization_barrier((both, codes))
    both = both.reshape(2, BLOCK_ROWS + 16, 128)
    params = both[:, BLOCK_ROWS : BLOCK_ROWS + 3 * CAP].reshape(2, 3, CAP, 1, 128)
    lin, quad, top = (params[:, k] for k in range(3))
    now = both[:, LOAD_ROWS:BLOCK_ROWS].reshape(2, CAP, S, 128)
    parts = ring_first(both[:, :BLOCK_ROWS].reshape(2 * BLOCK_ROWS, 128))
    low, high = (jnp.concatenate(parts[k : k + 2], axis=0) for k in (0, 2))
    low, high, codes = lax.optimization_barrier((low, high, codes))
    columns = pick(codes, ptdf)
    one_low, three_high = moved(low, "second", -1), moved(high, "second", -3)
    one_high, three_low = moved(high, "second", -1), moved(low, "second", -3)
    one_low, three_high, columns = lax.optimization_barrier((one_low, three_high, columns))
    two_low, two_high = moved(one_low, "second", -1), moved(three_high, "second", -3)
    load_part = slot_part = jnp.zeros((S, LINES_DEV), jnp.float32)
    for xs, starts in (
        ((low, high, one_low, three_high, one_high, three_low), (0, 4, 8, 28, 12, 24)),
        ((two_low, two_high), (16, 20)),
    ):
        load_part, slot_part = first_flow(
            load_part, slot_part, xs, columns, ptdf, block_of, starts
        )
    flow = load_part + slot_part

    bound = dual_step * flow_max
    line_price = line_price0
    for iteration in range(ITERS):
        last = iteration == ITERS - 1
        trial = line_price + dual_step * sum_bus(flow)
        price_next = trial - jnp.clip(trial, -bound, bound)
        reflected = 2.0 * price_next - line_price
        line_price = price_next
        three, two, one = slot_price(reflected, columns, (3, 2, 1))
        chunks = [*slot_price(reflected, columns, (0,)), one, two, three]
        unit = sum_z(sum_band(chunks), not last)
        unit = unit.reshape(-1, CAP, S, 128)
        k = unit.shape[0]
        before = now[:k]
        now = jnp.clip(
            (before - primal_step * (lin[:k] + unit)) / (1.0 + primal_step * quad[:k]),
            0.0,
            top[:k],
        )
        if not last:
            slots = gather_second(gather_first(now.reshape(2 * SLOT_ROWS, 128)))
            flow = load_part
            for r in (0, 1, 3, 2):
                flow = slot_flow(flow, slots[r], columns, r)
    slot_values = now[0]
    home = slot_values.reshape(CAP, S, N_BUS, N_BAND).transpose(2, 1, 0, 3)
    home = home.reshape(N_BUS, S, CAP * N_BAND)
    home = jnp.pad(home, ((0, 0), (0, 0), (0, 128 - CAP * N_BAND)))
    home = jnp.concatenate(exchange_bus([home[k] for k in range(N_BUS)]), axis=1)
    dispatch = exact_dot(home, where, NT)
    return dispatch, line_price


def solution(mesh):
    gens = P(("band", "bus"))
    in_specs = (
        P(None, ("band", "bus")),
        gens,
        gens,
        gens,
        gens,
        P(None, "bus", "band"),
        P("band", "bus"),
        P(None, "band"),
        P("band"),
    )
    out_specs = (P(None, ("band", "bus")), P(None, "band"))
    return jax.shard_map(
        on_device, mesh=mesh, in_specs=in_specs, out_specs=out_specs, check_vma=False
    )
```
